512 devices in a mesh: seq: 32 (over x, y), dp: 16 (over z, core).
Axes of the slice: x: 4, y: 8, z: 8, core: 2. Of those that a mesh axis runs over, the one named last changes fastest.
Arguments:
- input_rows: bfloat16 [16, 8192, 768], P('dp', 'seq'), may hold values from -6 to 6
- features: bfloat16 [16, 4096, 768], P('dp', 'seq'), may hold values from -36 to 36
- norm_gain: float32 [768], replicated, may hold values from 0.1 to 1.9
- w_query: bfloat16 [768, 512], replicated, may hold values from -3 to 3
- w_key: bfloat16 [768, 512], replicated, may hold values from -3 to 3
- w_value: bfloat16 [768, 512], replicated, may hold values from -0.21875 to 0.21875
- temper: float32 [4], replicated, may hold values from 1 to 4
- head_grads: bfloat16 [16, 4096, 512], P('dp', 'seq'), may hold values from -6 to 6
Outputs:
- feature_grad: bfloat16 [16, 4096, 768], P('dp', 'seq')
- conv_grad: float32 [3, 768, 768], P(None, 'seq')
The draws below stay inside these ranges and needn't reach their ends.
All inputs are finite; a program needn't handle non-finite values.
Results may differ from the reference program's by a relative error of at most 0.033.
Values may be sent and summed in bfloat16 or wider, within the bound.
A program may use at most 64 MiB of HBM per device.

```python
import math
import jax
import jax.numpy as jnp
from jax import lax

C = 768
HEADS = 4
HS = 128
KW = 3
TOK_DEV = 128
BATCH = 16
TOKENS = 4096
ROWS = 8192
N_SEQ = 32


def draw_features(key, part):
    key = jax.random.fold_in(key, 11)
    key_base, key_rows, key_cols = jax.random.split(key, 3)
    row_scale = jnp.exp(jax.random.uniform(key_rows, (BATCH, TOKENS, 1), jnp.float32, jnp.log(0.3), jnp.log(3.0)))
    col_scale = jnp.exp(jax.random.uniform(key_cols, (1, 1, C), jnp.float32, jnp.log(0.3), jnp.log(3.0)))
    base = jax.random.truncated_normal(key_base, -4.0, 4.0, (BATCH, TOKENS, C), jnp.float32)
    result = row_scale * col_scale * base
    return result.astype(jnp.bfloat16)


def draw_w_query(key, part):
    key = jax.random.fold_in(key, 23)
    key_base, key_cols = jax.random.split(key)
    col_scale = jnp.exp(jax.random.uniform(key_cols, (1, HEADS * HS), jnp.float32, jnp.log(0.3), jnp.log(3.0)))
    base = jax.random.truncated_normal(key_base, -4.0, 4.0, (C, HEADS * HS), jnp.float32)
    return (base * col_scale * C ** (-0.5)).astype(jnp.bfloat16)


def draw_w_key(key, part):
    key = jax.random.fold_in(key, 37)
    key_base, key_cols = jax.random.split(key)
    col_scale = jnp.exp(jax.random.uniform(key_cols, (1, HEADS * HS), jnp.float32, jnp.log(0.3), jnp.log(3.0)))
    base = jax.random.truncated_normal(key_base, -4.0, 4.0, (C, HEADS * HS), jnp.float32)
    return (base * col_scale * C ** (-0.5)).astype(jnp.bfloat16)


def raised(entries, stream_key, source, target, blocks, factor):
    def block_of(position):
        return (jnp.arange(entries.shape[position]) // (entries.shape[position] // blocks)).reshape((-1,) + (1,) * (entries.ndim - 1 - position))

    near = jax.random.permutation(stream_key, blocks)[block_of(target)]
    other_side = (block_of(target) + blocks // 2) % blocks
    return jnp.where((block_of(source) == near) | (block_of(source) == other_side), factor * entries, entries)


def shard_levels(own_key, dims, shards, least, top_value):
    def one(position, blocks):
        draws = jax.random.uniform(jax.random.fold_in(jax.random.fold_in(own_key, 6), position), (blocks,), jnp.float32, least / len(shards), top_value / len(shards))
        return jnp.repeat(jnp.exp(draws), dims[position] // blocks).reshape((-1,) + (1,) * (len(dims) - position - 1))

    loudness = one(*shards[0])
    for cut in shards[1:]:
        loudness = loudness * one(*cut)
    return loudness


def noise(key, extent, deviation, reach, cuts=(), held_as=jnp.bfloat16):
    level = shard_levels(key, extent, cuts, -0.22, 0.18) if cuts else 1.0
    values = jax.random.normal(key, extent, jnp.float32) * deviation * level
    return jnp.minimum(jnp.maximum(values, -reach), reach).astype(held_as)


def heavy_noise(key, dims, width, bound, cuts, heavy, held_as=jnp.bfloat16):
    array = width * jax.random.normal(key, dims, jnp.float32)
    if cuts:
        array = array * shard_levels(key, dims, cuts, -0.22, 0.18)
    return jnp.clip(raised(array, jax.random.fold_in(key, 3), *heavy), -bound, bound).astype(held_as)


def setup_inputs(seed: int = 0) -> dict:
    arg_keys = jax.random.split(jax.random.key(seed), 9)
    return {
        "input_rows": heavy_noise(arg_keys[0], (BATCH, ROWS, C), 1.0, 6.0, ((0, 16), (1, 32)), (1, 2, 32, 2.75)),
        "features": draw_features(jax.random.fold_in(arg_keys[8], 71), 0),
        "norm_gain": jnp.clip(1.0 + 0.18 * jax.random.normal(arg_keys[2], (C,), jnp.float32), 0.1, 1.9),
        "w_query": draw_w_query(jax.random.fold_in(arg_keys[8], 71), 0),
        "w_key": draw_w_key(jax.random.fold_in(arg_keys[8], 71), 0),
        "w_value": noise(arg_keys[5], (C, HEADS * HS), C ** -0.5, 0.21875),
        "temper": jnp.clip(jnp.exp(jax.random.uniform(arg_keys[6], (HEADS,), jnp.float32, math.log(1.0), math.log(4.0))), 1.0, 4.0),
        "head_grads": noise(arg_keys[7], (BATCH, TOKENS, HEADS * HS), 1.0, 6.0, ((0, 16), (1, 32))),
    }


EPSILON = 1e-06

def unit_rows(raw_vals):
    inv_scale = lax.rsqrt(lax.optimization_barrier(jnp.mean(raw_vals * raw_vals, axis=-1, keepdims=True)) + EPSILON)
    return (raw_vals * inv_scale, inv_scale)

def unit_back(upstream, unit_vals, inv_scale):
    return inv_scale * (upstream - unit_vals * lax.optimization_barrier(jnp.mean(unit_vals * upstream, axis=-1, keepdims=True)))

def block_partials(left, right):
    block_count = N_SEQ // HEADS
    span_rows = TOK_DEV // block_count
    left_blocks = left.reshape(N_SEQ, block_count, span_rows, TOKENS).astype(jnp.float32)
    right_blocks = right.reshape(N_SEQ, block_count, span_rows, HS).astype(jnp.float32)
    parts = jnp.einsum('rbsj,rbsd->bjd', left_blocks, right_blocks)
    rounded = lax.optimization_barrier(parts.astype(jnp.bfloat16))
    return lax.optimization_barrier(jnp.sum(rounded.astype(jnp.float32), axis=0))

def head_backward(operands):
    queries, keys_all, values, upstream, factor = operands
    scores = jnp.dot(queries, keys_all.T, preferred_element_type=jnp.float32) * factor
    expo_vals = jnp.exp(scores)
    attn_prob = expo_vals / lax.optimization_barrier(jnp.sum(expo_vals, axis=1, keepdims=True))
    prob_low = attn_prob.astype(jnp.bfloat16)
    grad_prob = jnp.dot(upstream, values.T, preferred_element_type=jnp.float32)
    grad_dot = lax.optimization_barrier(jnp.sum(attn_prob * grad_prob, axis=1, keepdims=True))
    grad_score = (attn_prob * (grad_prob - grad_dot) * factor).astype(jnp.bfloat16)
    grad_query = jnp.dot(grad_score, keys_all, preferred_element_type=jnp.float32)
    grad_query = lax.optimization_barrier(grad_query.astype(jnp.bfloat16)).astype(jnp.float32)
    grad_key = block_partials(grad_score, queries)
    grad_value = block_partials(prob_low, upstream)
    return (grad_query, grad_key, grad_value)

def reference(input_rows, features, norm_gain, w_query, w_key, w_value, temper, head_grads):
    factors = temper * (1.0 / math.sqrt(HS))

    def one_sequence(grad_total, operands):
        feature_rows, source_rows, upstream_rows = operands
        feat_vals = feature_rows.astype(jnp.float32)
        inv_rms = lax.rsqrt(lax.optimization_barrier(jnp.mean(feat_vals * feat_vals, axis=1, keepdims=True)) + EPSILON)
        normed = (feat_vals * inv_rms * norm_gain).astype(jnp.bfloat16)
        q_raw = jnp.dot(normed, w_query, preferred_element_type=jnp.float32).reshape(TOKENS, HEADS, HS)
        k_raw = jnp.dot(normed, w_key, preferred_element_type=jnp.float32).reshape(TOKENS, HEADS, HS)
        q_unit, q_scale = unit_rows(q_raw)
        k_unit, k_scale = unit_rows(k_raw)
        queries = q_unit.astype(jnp.bfloat16)
        keys_all = k_unit.astype(jnp.bfloat16)
        values = jnp.dot(normed, w_value, preferred_element_type=jnp.float32).astype(jnp.bfloat16)
        values = values.reshape(TOKENS, HEADS, HS)
        upstream = upstream_rows.reshape(TOKENS, HEADS, HS)
        grad_query, grad_key, grad_value = lax.map(head_backward, (jnp.transpose(queries, (1, 0, 2)), jnp.transpose(keys_all, (1, 0, 2)), jnp.transpose(values, (1, 0, 2)), jnp.transpose(upstream, (1, 0, 2)), factors))
        grad_query = jnp.transpose(grad_query, (1, 0, 2))
        grad_key = jnp.transpose(grad_key, (1, 0, 2))
        grad_value = jnp.transpose(grad_value, (1, 0, 2))
        dq_raw = unit_back(grad_query, q_unit, q_scale).astype(jnp.bfloat16).reshape(TOKENS, HEADS * HS)
        dk_raw = unit_back(grad_key, k_unit, k_scale).astype(jnp.bfloat16).reshape(TOKENS, HEADS * HS)
        dv_low = grad_value.astype(jnp.bfloat16).reshape(TOKENS, HEADS * HS)
        grad_normed = jnp.dot(dq_raw, w_query.T, preferred_element_type=jnp.float32)
        grad_normed = grad_normed + jnp.dot(dk_raw, w_key.T, preferred_element_type=jnp.float32)
        grad_normed = grad_normed + jnp.dot(dv_low, w_value.T, preferred_element_type=jnp.float32)
        gained = grad_normed * norm_gain
        unit_feats = feat_vals * inv_rms
        feature_grad = inv_rms * (gained - unit_feats * lax.optimization_barrier(jnp.mean(unit_feats * gained, axis=1, keepdims=True)))
        feature_grad = feature_grad.astype(jnp.bfloat16)
        padded = jnp.pad(source_rows, ((1, 1), (0, 0)))
        row_pairs = padded.reshape(TOKENS + 1, 2, C)
        windows = jnp.concatenate([row_pairs[:-1, 0], row_pairs[:-1, 1], row_pairs[1:, 0]], axis=1)
        grouped = windows.reshape(N_SEQ, TOK_DEV, KW * C).astype(jnp.float32)
        grads_grouped = feature_grad.reshape(N_SEQ, TOK_DEV, C).astype(jnp.float32)
        group_terms = jnp.einsum('gtc,gtd->gcd', grouped, grads_grouped) * (1.0 / BATCH)
        rounded = lax.optimization_barrier(group_terms.astype(jnp.bfloat16))
        return (grad_total + lax.optimization_barrier(jnp.sum(rounded.astype(jnp.float32), axis=0)), feature_grad)
    zero_total = jnp.zeros((KW * C, C), jnp.float32)
    grad_total, feature_grad = lax.scan(one_sequence, zero_total, (features, input_rows, head_grads))
    return (feature_grad, grad_total.reshape(KW, C, C))
```

```python
import math

import jax
import jax.numpy as jnp
from jax import lax
from jax.experimental import pallas as pl
from jax.experimental.pallas import tpu as pltpu
from jax.sharding import PartitionSpec as P

EPSILON = 1e-06
LAST_BOTH = (((1,), (1,)), ((), ()))
FIRST_BOTH = (((0,), (0,)), ((), ()))
MESH = pl.DeviceIdType.MESH
BF16, F32 = jnp.bfloat16, jnp.float32

NX, NY, NZ = 4, 8, 8
TOK, CH, HEADS, HS = 128, 768, 4, 128
QROWS = 512
SPAN = CH // (NX * NY)
PAD = 80
HALF = CH // 2


def unit_rows(raw):
    inv = lax.rsqrt(jnp.mean(raw * raw, axis=-1, keepdims=True) + EPSILON)
    return raw * inv, inv


def unit_back(upstream, unit, inv):
    return inv * (upstream - unit * jnp.mean(unit * upstream, axis=-1, keepdims=True))


def kernel(
    rows_ref, feat_ref, gain_ref, wq_ref, wk_ref, wv_ref, temper_ref, hg_ref,
    fg_out, cg_out,
    prev, okv, oqg, kv, qg, raw, wt, wbuf, e_buf, gp_buf, dkv, sib_in, stage, mid_in, end_in, back, total,
    dq_out, dq_back, dall, fgs, fgb, part, yb, tb, zb, fin, fin_sib,
    prev_sem, a_send, a_recv, q_send, q_recv, k_send, k_recv, w_send, w_recv,
    s_send, s_recv, m_send, m_recv, b_send, b_recv, g_send, g_recv, t_send, t_recv, z_send, z_recv, f_send, f_recv, c_sem,
):
    seq, dp = lax.axis_index("seq"), lax.axis_index("dp")
    x, y = lax.div(seq, NY), lax.rem(seq, NY)
    z, core = lax.div(dp, 2), lax.rem(dp, 2)
    n_seq = NX * NY
    xr, xl, xo = lax.rem(x + 1, NX), lax.rem(x + NX - 1, NX), lax.rem(x + 2, NX)
    sib = dp + 1 - 2 * core
    part_y, head = lax.rem(y, 2), lax.div(y, 2)
    me = 2 * x + core

    def at(xx, yy):
        return xx * NY + yy

    def copy(src, dst, send, recv, where):
        return pltpu.make_async_remote_copy(
            src_ref=src, dst_ref=dst, send_sem=send, recv_sem=recv, device_id=where, device_id_type=MESH
        )

    def arrived(dst, recv):
        copy(dst, dst, recv, recv, (seq, sib)).wait_recv()

    def rows_of(ref, start, size):
        return ref.at[pl.ds(pl.multiple_of(start, 16), size)]

    servers = [(at(x, 2 * i + core), 2 * z + 1 - lax.rem(y, 2)) for i in range(HEADS)]
    owners = [(at(x, 2 * j + 1 - core), 2 * z + part_y) for j in range(4)]
    ring_next, ring_prev = (lax.rem(seq + 1, n_seq), dp), (lax.rem(seq + n_seq - 1, n_seq), dp)
    right, left, twin, far = (at(xr, y), dp), (at(xl, y), dp), (seq, sib), (at(xo, y), dp)
    right_twin, left_twin = (at(xr, y), sib), (at(xl, y), sib)
    on_y = [(at(x, lax.rem(y + i, NY)), dp) for i in range(1, NY)]
    on_z = [(seq, lax.rem(dp + 2 * i, 2 * NZ)) for i in range(1, NZ)]

    barrier = pltpu.get_barrier_semaphore()
    partners = servers + owners + [ring_next, ring_prev, right, left, twin, far, right_twin, left_twin] + on_y + on_z
    for where in partners:
        pl.semaphore_signal(barrier, inc=1, device_id=where, device_id_type=MESH)

    feats = feat_ref[...].astype(F32)
    inv_rms = lax.rsqrt(jnp.mean(feats * feats, axis=1, keepdims=True) + EPSILON)
    gain = gain_ref[...]
    normed = (feats * inv_rms * gain).astype(BF16)
    raw[0] = jnp.dot(normed, wq_ref[...], preferred_element_type=F32)
    raw[1] = jnp.dot(normed, wk_ref[...], preferred_element_type=F32)
    values = jnp.dot(normed, wv_ref[...], preferred_element_type=F32).astype(BF16)
    for i in range(HEADS):
        cols = slice(i * HS, (i + 1) * HS)
        okv[i, :, 0:HS] = unit_rows(raw[1, :, cols])[0].astype(BF16)
        okv[i, :, HS:] = values[:, cols]
        oqg[i, :, 0:HS] = unit_rows(raw[0, :, cols])[0].astype(BF16)
        oqg[i, :, HS:] = hg_ref[:, cols]

    pl.semaphore_wait(barrier, len(partners))

    slot = lax.div(y, 2)
    their_me = 2 * x + 1 - lax.rem(y, 2)
    sends = []
    for i in range(HEADS):
        to_kv = kv.at[their_me, pl.ds(pl.multiple_of(slot * TOK, TOK), TOK)]
        sends.append(copy(okv.at[i], to_kv, a_send.at[i], a_recv.at[slot], servers[i]))
    for i in range(HEADS):
        sends.append(copy(oqg.at[i], rows_of(qg, slot * TOK, TOK), q_send.at[i], q_recv.at[slot], servers[i]))
    sends.append(copy(rows_ref.at[pl.ds(2 * TOK - 16, 16)], prev, prev_sem.at[0], prev_sem.at[1], ring_next))
    for one in sends:
        one.start()

    arrived(prev, prev_sem.at[1])
    row = lax.broadcasted_iota(jnp.int32, (2 * TOK, 3 * TOK), 0)
    lane = lax.broadcasted_iota(jnp.int32, (2 * TOK, 3 * TOK), 1)
    chosen = (row == 2 * lax.rem(lane, TOK) + lax.div(lane, TOK) - 1).astype(F32).astype(BF16)
    taps = lax.dot_general(rows_ref[...], chosen, FIRST_BOTH, preferred_element_type=F32)
    row = lax.broadcasted_iota(jnp.int32, (16, TOK), 0)
    lane = lax.broadcasted_iota(jnp.int32, (16, TOK), 1)
    first = ((row == 15) & (lane == 0) & (seq > 0)).astype(F32).astype(BF16)
    tap0 = taps[:, 0:TOK] + lax.dot_general(prev[...], first, FIRST_BOTH, preferred_element_type=F32)
    three = (tap0, taps[:, TOK : 2 * TOK], taps[:, 2 * TOK :])
    zeros = jnp.zeros((PAD - 3 * SPAN, TOK), F32)
    for i in range(NX):
        for j in range(NY):
            low = (i * NY + j) * SPAN
            block = jnp.concatenate([tap[low : low + SPAN] for tap in three] + [zeros], axis=0)
            wt[i, j * PAD : (j + 1) * PAD] = block.astype(BF16)

    def w_slot(xx, cc):
        return wbuf.at[:, pl.ds(pl.multiple_of((2 * xx + cc) * TOK, TOK), TOK)]

    def kv_quarter(block, j):
        return kv.at[block, pl.ds(j * TOK, TOK)]

    def kv_half(block, j):
        return kv.at[block, pl.ds(j * 2 * TOK, 2 * TOK)]

    from_left, from_right, from_far = 2 * xl + core, 2 * xr + core, 2 * xo + core
    for j in range(4):
        arrived(kv_quarter(me, j), a_recv.at[j])
        if j % 2:
            half = j // 2
            for i, (where, slot_at) in enumerate(((right, half), (left, 2 + half), (twin, 6 + half))):
                one = copy(kv_half(me, half), kv_half(me, half), k_send.at[3 * half + i], k_recv.at[slot_at], where)
                one.start()
                sends.append(one)
    for i, (block, slot_at, take, onward, far_at) in enumerate(
        ((from_left, 0, 0, right, 4), (from_right, 2, 1, left, 5))
    ):
        for half in range(2):
            arrived(kv_half(block, half), k_recv.at[slot_at + half])
            if half == take:
                one = copy(kv_half(block, half), kv_half(block, half), k_send.at[6 + i], k_recv.at[far_at], onward)
                one.start()
                sends.append(one)
        one = copy(kv.at[block], kv.at[block], k_send.at[8 + i], k_recv.at[8 + i], twin)
        one.start()
        sends.append(one)

    wbuf[:, pl.ds(pl.multiple_of(me * TOK, TOK), TOK)] = wt[x]
    for i, where in enumerate((right, left, far)):
        to_x = (xr, xl, xo)[i]
        one = copy(wt.at[to_x], w_slot(x, core), w_send.at[i], w_recv.at[i], where)
        one.start()
        sends.append(one)
    one = copy(wt.at[x], w_slot(x, core), w_send.at[3], w_recv.at[3], twin)
    one.start()
    sends.append(one)

    for j in range(4):
        arrived(rows_of(qg, j * TOK, TOK), q_recv.at[j])
    factor = temper_ref[head] * (1.0 / math.sqrt(HS))
    queries, upstream = qg[:, 0:HS], qg[:, HS:]

    def first_pass(block, sums):
        scores = lax.dot_general(kv[block, :, 0:HS], queries, LAST_BOTH, preferred_element_type=F32)
        expo = jnp.exp2(scores * (factor * math.log2(math.e)))
        e_buf[block] = expo
        grad_prob = lax.dot_general(kv[block, :, HS:], upstream, LAST_BOTH, preferred_element_type=F32)
        gp_buf[block] = grad_prob
        return (
            sums[0] + jnp.sum(expo, axis=0, keepdims=True),
            sums[1] + jnp.sum(expo * grad_prob, axis=0, keepdims=True),
        )

    sums = (jnp.zeros((1, QROWS), F32), jnp.zeros((1, QROWS), F32))
    sums = first_pass(me, sums)
    for half in range(2):
        arrived(kv_half(me + 1 - 2 * core, half), k_recv.at[6 + half])
    sums = first_pass(me + 1 - 2 * core, sums)
    sums = first_pass(from_left, sums)
    sums = first_pass(from_right, sums)
    arrived(kv_half(from_far, 0), k_recv.at[4])
    arrived(kv_half(from_far, 1), k_recv.at[5])
    one = copy(kv.at[from_far], kv.at[from_far], k_send.at[10], k_recv.at[10], twin)
    one.start()
    sends.append(one)
    for i, other in enumerate((2 * xl + 1 - core, 2 * xr + 1 - core)):
        arrived(kv.at[other], k_recv.at[8 + i])
        sums = first_pass(other, sums)
    sums = first_pass(from_far, sums)
    far_other = 2 * xo + 1 - core
    arrived(kv.at[far_other], k_recv.at[10])
    sums = first_pass(far_other, sums)

    for i, from_x in enumerate((xl, xr, xo)):
        arrived(w_slot(from_x, core), w_recv.at[i])
        one = copy(w_slot(from_x, core), w_slot(from_x, core), w_send.at[4 + i], w_recv.at[4 + i], twin)
        one.start()
        sends.append(one)

    inv_sum = 1.0 / sums[0]
    grad_dot = sums[1] * inv_sum

    def second_pass(block, grad_query):
        prob = e_buf[block] * inv_sum
        grad_score = (prob * ((gp_buf[block] - grad_dot) * factor)).astype(BF16)
        dkv[block, :, HS:] = jnp.dot(prob.astype(BF16), upstream, preferred_element_type=F32).astype(BF16)
        dkv[block, :, 0:HS] = jnp.dot(grad_score, queries, preferred_element_type=F32).astype(BF16)
        keys_t = jnp.transpose(kv[block, :, 0:HS])
        return grad_query + jnp.dot(keys_t, grad_score, preferred_element_type=F32)

    grad_query = jnp.zeros((HS, QROWS), F32)
    half_rows = QROWS // 2
    for i, to_x in enumerate((xo, xr, xl, x)):
        grad_query = second_pass(2 * to_x + 1 - core, grad_query)
        one = copy(dkv.at[2 * to_x + 1 - core], sib_in.at[i], s_send.at[i], s_recv.at[i], twin)
        one.start()
        sends.append(one)
        grad_query = second_pass(2 * to_x + core, grad_query)
        if i == 3:
            dq_out[...] = jnp.transpose(grad_query).astype(BF16)
            for j in range(4):
                one = copy(
                    dq_out.at[pl.ds(j * TOK, TOK)], dq_back.at[head], b_send.at[j], b_recv.at[head], owners[j]
                )
                one.start()
                sends.append(one)
        arrived(sib_in.at[i], s_recv.at[i])
        summed = dkv[2 * to_x + core].astype(F32) + sib_in[i].astype(F32)
        if i == 0:
            stage[0] = summed.astype(BF16)
            for k, where in enumerate((right, left)):
                src = stage.at[0, pl.ds(k * half_rows, half_rows)]
                one = copy(src, mid_in.at[k], m_send.at[k], m_recv.at[k], where)
                one.start()
                sends.append(one)
        elif i < 3:
            k = i - 1
            arrived(mid_in.at[k], m_recv.at[k])
            both = (summed[0:half_rows], summed[half_rows:])
            mine = both[k] + mid_in[k].astype(F32)
            stage[i, k * half_rows : (k + 1) * half_rows] = mine.astype(BF16)
            stage[i, (1 - k) * half_rows : (2 - k) * half_rows] = both[1 - k].astype(BF16)
            one = copy(stage.at[i], end_in.at[k], m_send.at[2 + k], m_recv.at[2 + k], (right, left)[k])
            one.start()
            sends.append(one)
        else:
            for k in range(2):
                arrived(end_in.at[k], m_recv.at[2 + k])
            total[...] = (summed + end_in[0].astype(F32) + end_in[1].astype(F32)).astype(BF16)
            for j in range(4):
                src = total.at[pl.ds(j * TOK, TOK)]
                one = copy(src, back.at[head], b_send.at[4 + j], b_recv.at[4 + head], owners[j])
                one.start()
                sends.append(one)

    def put_raw_grad(which, i, upstream_grad):
        unit, inv = unit_rows(raw[which, :, i * HS : (i + 1) * HS])
        dall[which, :, i * HS : (i + 1) * HS] = unit_back(upstream_grad.astype(F32), unit, inv).astype(BF16)

    for i in range(HEADS):
        arrived(dq_back.at[i], b_recv.at[i])
        put_raw_grad(0, i, dq_back[i])
    grad_normed = lax.dot_general(dall[0], wq_ref[...], LAST_BOTH, preferred_element_type=F32)
    for i in range(HEADS):
        arrived(back.at[i], b_recv.at[4 + i])
        put_raw_grad(1, i, back[i, :, 0:HS])
        dall[2, :, i * HS : (i + 1) * HS] = back[i, :, HS:]
    grad_normed += lax.dot_general(dall[1], wk_ref[...], LAST_BOTH, preferred_element_type=F32)
    grad_normed += lax.dot_general(dall[2], wv_ref[...], LAST_BOTH, preferred_element_type=F32)
    gained = grad_normed * gain
    unit_feats = feats * inv_rms
    feature_grad = inv_rms * (gained - unit_feats * jnp.mean(unit_feats * gained, axis=1, keepdims=True))
    feature_grad = feature_grad.astype(BF16)
    fg_out[...] = feature_grad
    fgs[0] = feature_grad[:, 0:HALF]
    fgs[1] = feature_grad[:, HALF:]

    def g_slot(xx, cc):
        return rows_of(fgb, (2 * xx + cc) * TOK, TOK)

    fgb[pl.ds(pl.multiple_of(me * TOK, TOK), TOK)] = fgs[core]
    for i, (where, cc, slot_at) in enumerate(
        (
            (right, core, core),
            (left, core, 2 + core),
            (right_twin, 1 - core, core),
            (left_twin, 1 - core, 2 + core),
            (twin, 1 - core, 6),
        )
    ):
        one = copy(fgs.at[cc], g_slot(x, core), g_send.at[i], g_recv.at[slot_at], where)
        one.start()
        sends.append(one)
    arrived(g_slot(xl, 0), g_recv.at[0])
    one = copy(g_slot(xl, 0), g_slot(xl, 0), g_send.at[5], g_recv.at[4], right)
    one.start()
    sends.append(one)
    arrived(g_slot(xr, 1), g_recv.at[3])
    one = copy(g_slot(xr, 1), g_slot(xr, 1), g_send.at[6], g_recv.at[5], left)
    one.start()
    sends.append(one)
    for i, from_x in enumerate((xl, xr, xo)):
        arrived(w_slot(from_x, 1 - core), w_recv.at[4 + i])
    arrived(w_slot(x, 1 - core), w_recv.at[3])
    arrived(g_slot(xl, 1), g_recv.at[1])
    arrived(g_slot(xr, 0), g_recv.at[2])
    arrived(g_slot(x, 1 - core), g_recv.at[6])
    arrived(g_slot(xo, 0), g_recv.at[4])
    arrived(g_slot(xo, 1), g_recv.at[5])
    part[...] = (jnp.dot(wbuf[...], fgb[...], preferred_element_type=F32) * (1.0 / (2 * NZ))).astype(BF16)

    yb[y] = part[pl.ds(pl.multiple_of(y * PAD, 16), PAD)]
    for i in range(1, NY):
        to_y = lax.rem(y + i, NY)
        one = copy(rows_of(part, to_y * PAD, PAD), yb.at[y], t_send.at[i - 1], t_recv.at[y], on_y[i - 1])
        one.start()
        sends.append(one)
    for i in range(1, NY):
        from_y = lax.rem(y + i, NY)
        arrived(yb.at[from_y], t_recv.at[from_y])
    block = yb[0].astype(F32)
    for i in range(1, NY):
        block += yb[i].astype(F32)

    for i in range(PAD // 16):
        for j in range(HALF // 128):
            tb[3 * i + j] = block[16 * i : 16 * (i + 1), 128 * j : 128 * (j + 1)].astype(BF16)
    tb[15] = jnp.zeros((16, 128), BF16)
    zb[z] = tb[pl.ds(2 * z, 2)]
    for i in range(1, NZ):
        to_z = lax.rem(z + i, NZ)
        one = copy(tb.at[pl.ds(2 * to_z, 2)], zb.at[z], z_send.at[i - 1], z_recv.at[z], on_z[i - 1])
        one.start()
        sends.append(one)
    for i in range(1, NZ):
        from_z = lax.rem(z + i, NZ)
        arrived(zb.at[from_z], z_recv.at[from_z])
    tiles = zb[0].astype(F32)
    for i in range(1, NZ):
        tiles += zb[i].astype(F32)
    fin[pl.ds(2 * z, 2)] = tiles
    for i in range(1, NZ):
        mine = fin.at[pl.ds(2 * z, 2)]
        one = copy(mine, mine, f_send.at[i - 1], f_recv.at[z], on_z[i - 1])
        one.start()
        sends.append(one)
    for i in range(1, NZ):
        from_z = lax.rem(z + i, NZ)
        arrived(fin.at[pl.ds(2 * from_z, 2)], f_recv.at[from_z])
    one = copy(fin, fin_sib, c_sem.at[0], c_sem.at[1], twin)
    one.start()
    sends.append(one)
    arrived(fin_sib, c_sem.at[1])
    own, other = fin[...], fin_sib[...]
    for half in range(2):
        mine = jnp.where(core == half, own, other)
        wide = [jnp.concatenate([mine[3 * i + j] for j in range(3)], axis=1) for i in range(PAD // 16)]
        wide = jnp.concatenate(wide, axis=0)
        for k in range(3):
            cg_out[k, :, half * HALF : (half + 1) * HALF] = wide[k * SPAN : (k + 1) * SPAN]

    for one in sends:
        one.wait_send()


def on_device(input_rows, features, norm_gain, w_query, w_key, w_value, temper, head_grads):
    vmem = pl.BlockSpec(memory_space=pltpu.VMEM)
    dma = pltpu.SemaphoreType.DMA

    def scratch(*shape, dtype=BF16):
        return pltpu.VMEM(shape, dtype)

    fg, cg = pl.pallas_call(
        kernel,
        out_shape=(
            jax.ShapeDtypeStruct((TOK, CH), BF16),
            jax.ShapeDtypeStruct((3, SPAN, CH), F32),
        ),
        in_specs=[vmem] * 6 + [pl.BlockSpec(memory_space=pltpu.SMEM), vmem],
        out_specs=(vmem, vmem),
        scratch_shapes=[
            scratch(16, CH),
            scratch(HEADS, TOK, 2 * HS),
            scratch(HEADS, TOK, 2 * HS),
            scratch(8, QROWS, 2 * HS),
            scratch(QROWS, 2 * HS),
            scratch(2, TOK, HEADS * HS, dtype=F32),
            scratch(NX, NY * PAD, TOK),
            scratch(NY * PAD, 8 * TOK),
            scratch(8, QROWS, QROWS, dtype=F32),
            scratch(8, QROWS, QROWS, dtype=F32),
            scratch(8, QROWS, 2 * HS),
            scratch(NX, QROWS, 2 * HS),
            scratch(3, QROWS, 2 * HS),
            scratch(2, QROWS // 2, 2 * HS),
            scratch(2, QROWS, 2 * HS),
            scratch(HEADS, TOK, 2 * HS),
            scratch(QROWS, 2 * HS),
            scratch(QROWS, HS),
            scratch(HEADS, TOK, HS),
            scratch(3, TOK, HEADS * HS),
            scratch(2, TOK, HALF),
            scratch(8 * TOK, HALF),
            scratch(NY * PAD, HALF),
            scratch(NY, PAD, HALF),
            scratch(16, 16, 128),
            scratch(NZ, 2, 16, 128),
            scratch(16, 16, 128, dtype=F32),
            scratch(16, 16, 128, dtype=F32),
            dma((2,)),
            dma((4,)), dma((4,)),
            dma((4,)), dma((4,)),
            dma((11,)), dma((11,)),
            dma((7,)), dma((7,)),
            dma((4,)), dma((4,)),
            dma((4,)), dma((4,)),
            dma((8,)), dma((8,)),
            dma((7,)), dma((7,)),
            dma((7,)), dma((8,)),
            dma((7,)), dma((8,)),
            dma((7,)), dma((8,)),
            dma((2,)),
        ],
        compiler_params=pltpu.CompilerParams(
            collective_id=0, has_side_effects=True, vmem_limit_bytes=56 * 1024 * 1024
        ),
    )(
        input_rows[0], features[0], norm_gain.reshape(1, CH), w_query, w_key, w_value, temper, head_grads[0],
    )
    return fg[None], cg


def solution(mesh):
    return jax.shard_map(
        on_device,
        mesh=mesh,
        in_specs=(
            P("dp", "seq", None),
            P("dp", "seq", None),
            P(),
            P(),
            P(),
            P(),
            P(),
            P("dp", "seq", None),
        ),
        out_specs=(P("dp", "seq", None), P(None, "seq", None)),
        check_vma=False,
    )
```

```python
import math

import jax
import jax.numpy as jnp
from jax import lax
from jax.experimental import pallas as pl
from jax.experimental.pallas import tpu as pltpu
from jax.sharding import PartitionSpec as P

EPSILON = 1e-06
LAST_BOTH = (((1,), (1,)), ((), ()))
FIRST_BOTH = (((0,), (0,)), ((), ()))
MESH = pl.DeviceIdType.MESH
BF16, F32 = jnp.bfloat16, jnp.float32

NX, NY, NZ = 4, 8, 8
TOK, CH, HEADS, HS = 128, 768, 4, 128
QROWS = 512
SPAN = CH // (NX * NY)
PAD = 80
HALF = CH // 2


def unit_rows(raw):
    inv = lax.rsqrt(jnp.mean(raw * raw, axis=-1, keepdims=True) + EPSILON)
    return raw * inv, inv


def unit_back(upstream, unit, inv):
    return inv * (upstream - unit * jnp.mean(unit * upstream, axis=-1, keepdims=True))


def kernel(
    rows_ref, feat_ref, gain_ref, wq_ref, wk_ref, wv_ref, temper_ref, hg_ref,
    fg_out, cg_out,
    prev, outgoing, keys, vals, qg, raw, wt, wbuf, e_buf, gp_buf, dv, dk, sib_v, sib_k, st_v, st_k, in_v, in_k,
    total, back, dall, fgs, fgb, part, yb1, zb1, s1, s2, zb2, yb2, fin, fin_sib,
    prev_sem, a_send, a_recv, k_send, k_recv, w_send, w_recv, sv_send, sv_recv, sk_send, sk_recv,
    mv_send, mv_recv, mk_send, mk_recv, b_send, b_recv, g_send, g_recv, t_send, t_recv, u_send, u_recv, f_send, f_recv, c_sem,
):
    seq, dp = lax.axis_index("seq"), lax.axis_index("dp")
    x, y = lax.div(seq, NY), lax.rem(seq, NY)
    z, core = lax.div(dp, 2), lax.rem(dp, 2)
    n_seq = NX * NY
    xr, xl, xo = lax.rem(x + 1, NX), lax.rem(x + NX - 1, NX), lax.rem(x + 2, NX)
    sib = dp + 1 - 2 * core
    part_y, head = lax.rem(y, 2), lax.div(y, 2)
    me = 2 * x + core

    def at(xx, yy):
        return xx * NY + yy

    def copy(src, dst, send, recv, where):
        return pltpu.make_async_remote_copy(
            src_ref=src, dst_ref=dst, send_sem=send, recv_sem=recv, device_id=where, device_id_type=MESH
        )

    sends = []

    def send(src, dst, send_sem, recv_sem, where):
        one = copy(src, dst, send_sem, recv_sem, where)
        one.start()
        sends.append(one)
        return one

    def arrived(dst, recv):
        copy(dst, dst, recv, recv, (seq, sib)).wait_recv()

    def rows_of(ref, start, size):
        return ref.at[pl.ds(pl.multiple_of(start, 16), size)]

    servers = [(at(x, 2 * i + core), 2 * z + 1 - lax.rem(y, 2)) for i in range(HEADS)]
    owners = [(at(x, 2 * j + 1 - core), 2 * z + part_y) for j in range(4)]
    ring_next, ring_prev = (lax.rem(seq + 1, n_seq), dp), (lax.rem(seq + n_seq - 1, n_seq), dp)
    right, left, twin, far = (at(xr, y), dp), (at(xl, y), dp), (seq, sib), (at(xo, y), dp)
    right_twin, left_twin = (at(xr, y), sib), (at(xl, y), sib)
    on_y = [(at(x, lax.rem(y + i, NY)), dp) for i in range(1, NY)]
    on_z = [(seq, lax.rem(dp + 2 * i, 2 * NZ)) for i in range(1, NZ)]

    barrier = pltpu.get_barrier_semaphore()
    partners = servers + owners + [ring_next, ring_prev, right, left, twin, far, right_twin, left_twin] + on_y + on_z
    for where in partners:
        pl.semaphore_signal(barrier, inc=1, device_id=where, device_id_type=MESH)

    feats = feat_ref[...].astype(F32)
    inv_rms = lax.rsqrt(jnp.mean(feats * feats, axis=1, keepdims=True) + EPSILON)
    gain = gain_ref[...]
    normed = (feats * inv_rms * gain).astype(BF16)
    slot = lax.div(y, 2)
    their_me = 2 * x + 1 - lax.rem(y, 2)

    def start_heads(kind, to):
        started = []
        for i in range(HEADS):
            started.append(copy(outgoing.at[kind, i], to, a_send.at[kind, i], a_recv.at[kind, slot], servers[i]))
            started[i].start()
        return started

    def wait_heads(started):
        for one in started:
            one.wait_send()

    def project(which, w_ref):
        raw[which] = jnp.dot(normed, w_ref[...], preferred_element_type=F32)
        for i in range(HEADS):
            outgoing[which, i] = unit_rows(raw[which, :, i * HS : (i + 1) * HS])[0].astype(BF16)

    project(0, wk_ref)
    pl.semaphore_wait(barrier, len(partners))
    slot_rows = pl.ds(pl.multiple_of(slot * TOK, TOK), TOK)
    sent = start_heads(0, keys.at[their_me, slot_rows])
    send(rows_ref.at[pl.ds(2 * TOK - 16, 16)], prev, prev_sem.at[0], prev_sem.at[1], ring_next)
    project(1, wq_ref)
    values = jnp.dot(normed, wv_ref[...], preferred_element_type=F32).astype(BF16)
    for i in range(HEADS):
        outgoing[2, i] = values[:, i * HS : (i + 1) * HS]
        outgoing[3, i] = hg_ref[:, i * HS : (i + 1) * HS]
    wait_heads(sent)
    sent = start_heads(1, qg.at[0, slot_rows])

    arrived(prev, prev_sem.at[1])
    row = lax.broadcasted_iota(jnp.int32, (2 * TOK, 3 * TOK), 0)
    lane = lax.broadcasted_iota(jnp.int32, (2 * TOK, 3 * TOK), 1)
    chosen = (row == 2 * lax.rem(lane, TOK) + lax.div(lane, TOK) - 1).astype(F32).astype(BF16)
    taps = lax.dot_general(rows_ref[...], chosen, FIRST_BOTH, preferred_element_type=F32)
    row = lax.broadcasted_iota(jnp.int32, (16, TOK), 0)
    lane = lax.broadcasted_iota(jnp.int32, (16, TOK), 1)
    first = ((row == 15) & (lane == 0) & (seq > 0)).astype(F32).astype(BF16)
    tap0 = taps[:, 0:TOK] + lax.dot_general(prev[...], first, FIRST_BOTH, preferred_element_type=F32)
    three = (tap0, taps[:, TOK : 2 * TOK], taps[:, 2 * TOK :])
    zeros = jnp.zeros((PAD - 3 * SPAN, TOK), F32)
    for i in range(NX):
        for j in range(NY):
            low = (i * NY + j) * SPAN
            block = jnp.concatenate([tap[low : low + SPAN] for tap in three] + [zeros], axis=0)
            wt[i, j * PAD : (j + 1) * PAD] = block.astype(BF16)

    def chunk(ref, block, i):
        j = lax.rem(slot + (0, 1, 3, 2)[i], 4)
        return ref.at[block, pl.ds(pl.multiple_of(j * TOK, TOK), TOK)], j

    from_left, from_right, from_far = 2 * xl + core, 2 * xr + core, 2 * xo + core
    twin_me, twin_left, twin_right, twin_far = me + 1 - 2 * core, 2 * xl + 1 - core, 2 * xr + 1 - core, 2 * xo + 1 - core
    both = (keys, vals)

    def ring_own(t, i):
        mine, j = chunk(both[t], me, i)
        arrived(mine, a_recv.at[2 * t, j])
        for k, where in enumerate((right, left, twin)):
            send(mine, mine, k_send.at[t, 3 * i + k], k_recv.at[t, (0, 4, 12)[k] + i], where)

    def ring_on(t):
        for i, block, first_slot, onward in (
            (0, from_left, 0, right), (1, from_left, 0, right), (0, from_right, 4, None), (1, from_right, 4, None),
            (2, from_right, 4, left), (3, from_right, 4, left), (2, from_left, 0, None), (3, from_left, 0, None),
        ):
            piece, _ = chunk(both[t], block, i)
            arrived(piece, k_recv.at[t, first_slot + i])
            if onward is not None:
                send(piece, piece, k_send.at[t, 12 + i], k_recv.at[t, 8 + i], onward)
        for k, block in enumerate((from_left, from_right)):
            send(both[t].at[block], both[t].at[block], k_send.at[t, 16 + k], k_recv.at[t, 16 + k], twin)

    def ring_far(t):
        for i in range(4):
            arrived(chunk(both[t], from_far, i)[0], k_recv.at[t, 8 + i])
        send(both[t].at[from_far], both[t].at[from_far], k_send.at[t, 18], k_recv.at[t, 18], twin)

    def got_twin(t):
        for i in range(4):
            arrived(chunk(both[t], twin_me, i)[0], k_recv.at[t, 12 + i])

    def got_from_twin(t, k):
        arrived(both[t].at[(twin_left, twin_right, twin_far)[k]], k_recv.at[t, 16 + k])

    ring_own(0, 0)
    ring_own(0, 1)
    wait_heads(sent)
    sent = start_heads(2, vals.at[their_me, slot_rows])
    ring_own(0, 2)
    ring_own(0, 3)
    wait_heads(sent)
    sends += start_heads(3, qg.at[1, slot_rows])
    ring_on(0)

    for j in range(4):
        arrived(qg.at[0, pl.ds(j * TOK, TOK)], a_recv.at[1, j])
    factor = temper_ref[head] * (1.0 / math.sqrt(HS))

    def score_pass(block, exp_sum):
        scores = lax.dot_general(keys[block], qg[0], LAST_BOTH, preferred_element_type=F32)
        expo = jnp.exp2(scores * (factor * math.log2(math.e)))
        e_buf[block] = expo
        return exp_sum + jnp.sum(expo, axis=0, keepdims=True)

    exp_sum = score_pass(me, jnp.zeros((1, QROWS), F32))
    ring_own(1, 0)
    got_twin(0)
    exp_sum = score_pass(twin_me, exp_sum)
    ring_own(1, 1)
    exp_sum = score_pass(from_left, exp_sum)
    ring_own(1, 2)
    exp_sum = score_pass(from_right, exp_sum)
    ring_own(1, 3)
    ring_far(0)
    got_from_twin(0, 0)
    exp_sum = score_pass(twin_left, exp_sum)
    got_from_twin(0, 1)
    exp_sum = score_pass(twin_right, exp_sum)
    ring_on(1)
    exp_sum = score_pass(from_far, exp_sum)
    got_from_twin(0, 2)
    exp_sum = score_pass(twin_far, exp_sum)
    inv_sum = 1.0 / exp_sum

    for j in range(4):
        arrived(qg.at[1, pl.ds(j * TOK, TOK)], a_recv.at[3, j])
    order = (xo, xr, xl, x)
    to = (far, right, left)

    def value_grad(block):
        prob = (e_buf[block] * inv_sum).astype(BF16)
        dv[block] = jnp.dot(prob, qg[1], preferred_element_type=F32).astype(BF16)

    def prob_grad(block, dot_sum):
        grad_prob = lax.dot_general(vals[block], qg[1], LAST_BOTH, preferred_element_type=F32)
        gp_buf[block] = grad_prob
        return dot_sum + jnp.sum(e_buf[block] * grad_prob, axis=0, keepdims=True)

    def pass_values(i):
        arrived(sib_v.at[i], sv_recv.at[i])
        st_v[i] = (dv[2 * order[i] + core].astype(F32) + sib_v[i].astype(F32)).astype(BF16)
        send(st_v.at[i], in_v.at[i], mv_send.at[i], mv_recv.at[i], to[i])

    dot_sum = jnp.zeros((1, QROWS), F32)
    for i in range(NX):
        block = 2 * order[i] + 1 - core
        value_grad(block)
        send(dv.at[block], sib_v.at[i], sv_send.at[i], sv_recv.at[i], twin)
        value_grad(2 * order[i] + core)
        if i > 0:
            pass_values(i - 1)
        if i == 0:
            dot_sum = prob_grad(me, dot_sum)
            got_twin(1)
            dot_sum = prob_grad(twin_me, dot_sum)
        elif i == 1:
            dot_sum = prob_grad(from_left, dot_sum)
            dot_sum = prob_grad(from_right, dot_sum)
            ring_far(1)
        elif i == 2:
            for k, other in enumerate((twin_left, twin_right)):
                got_from_twin(1, k)
                dot_sum = prob_grad(other, dot_sum)
        else:
            dot_sum = prob_grad(from_far, dot_sum)
            got_from_twin(1, 2)
            dot_sum = prob_grad(twin_far, dot_sum)

    grad_dot = dot_sum * inv_sum
    inv_factor = inv_sum * factor
    half_rows = QROWS // 2

    def key_grad(block, half, grad_query):
        low = half * half_rows
        high = low + half_rows
        grad_score = (e_buf[block, low:high] * inv_factor * (gp_buf[block, low:high] - grad_dot)).astype(BF16)
        dk[block, low:high] = jnp.dot(grad_score, qg[0], preferred_element_type=F32).astype(BF16)
        keys_t = jnp.transpose(keys[block, low:high])
        return grad_query + jnp.dot(keys_t, grad_score, preferred_element_type=F32)

    def half_of(ref, i, half):
        return ref.at[i, pl.ds(half * half_rows, half_rows)]

    def pass_keys(half, i):
        low = half * half_rows
        high = low + half_rows
        arrived(half_of(sib_k, i, half), sk_recv.at[half, i])
        summed = dk[2 * order[i] + core, low:high].astype(F32) + sib_k[i, low:high].astype(F32)
        if i < 3:
            st_k[i, low:high] = summed.astype(BF16)
            send(half_of(st_k, i, half), half_of(in_k, i, half), mk_send.at[half, i], mk_recv.at[half, i], to[i])
        return summed

    grad_query = jnp.zeros((HS, QROWS), F32)
    pending = None
    for half in range(2):
        for i in range(NX):
            block = 2 * order[i] + 1 - core
            grad_query = key_grad(block, half, grad_query)
            send(half_of(dk, block, half), half_of(sib_k, i, half), sk_send.at[half, i], sk_recv.at[half, i], twin)
            grad_query = key_grad(2 * order[i] + core, half, grad_query)
            if pending is not None and pending[1] < 3:
                pass_keys(*pending)
            pending = (half, i)
    total[0] = jnp.transpose(grad_query).astype(BF16)

    def start_back(kind, j):
        src = total.at[kind, pl.ds(j * TOK, TOK)]
        send(src, back.at[kind, head], b_send.at[kind, j], b_recv.at[kind, head], owners[j])

    for j in range(4):
        start_back(0, j)
    arrived(sib_v.at[3], sv_recv.at[3])
    summed = dv[me].astype(F32) + sib_v[3].astype(F32)
    for i in range(3):
        arrived(in_v.at[i], mv_recv.at[i])
        summed += in_v[i].astype(F32)
    total[2] = summed.astype(BF16)
    for j in range(4):
        start_back(2, j)
    for half in range(2):
        low = half * half_rows
        high = low + half_rows
        summed = pass_keys(half, 3)
        for i in range(3):
            arrived(half_of(in_k, i, half), mk_recv.at[half, i])
            summed += in_k[i, low:high].astype(F32)
        total[1, low:high] = summed.astype(BF16)
        for j in range(2 * half, 2 * half + 2):
            start_back(1, j)

    def w_slot(xx, cc):
        return wbuf.at[:, pl.ds(pl.multiple_of((2 * xx + cc) * TOK, TOK), TOK)]

    for i, where in enumerate((right, left, far)):
        send(wt.at[(xr, xl, xo)[i]], w_slot(x, core), w_send.at[i], w_recv.at[i], where)
    send(wt.at[x], w_slot(x, core), w_send.at[3], w_recv.at[3], twin)
    wbuf[:, pl.ds(pl.multiple_of(me * TOK, TOK), TOK)] = wt[x]

    def put_raw_grad(which, i, upstream_grad):
        unit, inv = unit_rows(raw[1 - which, :, i * HS : (i + 1) * HS])
        dall[which, :, i * HS : (i + 1) * HS] = unit_back(upstream_grad.astype(F32), unit, inv).astype(BF16)

    for i in range(HEADS):
        arrived(back.at[0, i], b_recv.at[0, i])
        put_raw_grad(0, i, back[0, i])
    grad_normed = lax.dot_general(dall[0], wq_ref[...], LAST_BOTH, preferred_element_type=F32)
    for i in range(HEADS):
        arrived(back.at[2, i], b_recv.at[2, i])
        dall[2, :, i * HS : (i + 1) * HS] = back[2, i]
    grad_normed += lax.dot_general(dall[2], wv_ref[...], LAST_BOTH, preferred_element_type=F32)
    for i in range(HEADS):
        arrived(back.at[1, i], b_recv.at[1, i])
        put_raw_grad(1, i, back[1, i])
    grad_normed += lax.dot_general(dall[1], wk_ref[...], LAST_BOTH, preferred_element_type=F32)
    gained = grad_normed * gain
    unit_feats = feats * inv_rms
    feature_grad = inv_rms * (gained - unit_feats * jnp.mean(unit_feats * gained, axis=1, keepdims=True))
    feature_grad = feature_grad.astype(BF16)
    fg_out[...] = feature_grad
    fgs[0] = feature_grad[:, 0:HALF]
    fgs[1] = feature_grad[:, HALF:]

    def g_slot(xx, cc):
        return rows_of(fgb, (2 * xx + cc) * TOK, TOK)

    for i, (where, cc, slot_at) in enumerate(
        (
            (right, core, core),
            (left, core, 2 + core),
            (right_twin, 1 - core, core),
            (left_twin, 1 - core, 2 + core),
            (twin, 1 - core, 6),
        )
    ):
        send(fgs.at[cc], g_slot(x, core), g_send.at[i], g_recv.at[slot_at], where)
    fgb[pl.ds(pl.multiple_of(me * TOK, TOK), TOK)] = fgs[core]
    for i, from_x in enumerate((xr, xl, xo)):
        arrived(w_slot((xl, xr, xo)[i], core), w_recv.at[i])
        send(w_slot((xl, xr, xo)[i], core), w_slot((xl, xr, xo)[i], core), w_send.at[4 + i], w_recv.at[4 + i], twin)
    arrived(g_slot(xl, 0), g_recv.at[0])
    send(g_slot(xl, 0), g_slot(xl, 0), g_send.at[5], g_recv.at[4], right)
    arrived(g_slot(xr, 1), g_recv.at[3])
    send(g_slot(xr, 1), g_slot(xr, 1), g_send.at[6], g_recv.at[5], left)
    arrived(w_slot(x, 1 - core), w_recv.at[3])
    for i in range(3):
        arrived(w_slot((xl, xr, xo)[i], 1 - core), w_recv.at[4 + i])
    arrived(g_slot(xl, 1), g_recv.at[1])
    arrived(g_slot(xr, 0), g_recv.at[2])
    arrived(g_slot(x, 1 - core), g_recv.at[6])
    arrived(g_slot(xo, 0), g_recv.at[4])
    arrived(g_slot(xo, 1), g_recv.at[5])
    terms = jnp.dot(wbuf[...], fgb[...], preferred_element_type=F32) * (1.0 / (2 * NZ))
    for b in range(NY):
        for i in range(PAD // 16):
            for j in range(HALF // 128):
                low = b * PAD + 16 * i
                part[b, 3 * i + j] = terms[low : low + 16, 128 * j : 128 * (j + 1)].astype(BF16)
        part[b, 15] = jnp.zeros((16, 128), BF16)

    def added(ref):
        out = ref[0].astype(F32)
        for i in range(1, 8):
            out += ref[i].astype(F32)
        return out

    for i in range(1, 8):
        to_y, to_z = lax.rem(y + i, NY), lax.rem(z + i, NZ)
        send(part.at[to_y, pl.ds(0, 8)], yb1.at[y], t_send.at[0, i], t_recv.at[0, y], on_y[i - 1])
        send(part.at[:, 8 + to_z], zb1.at[z], t_send.at[1, i], t_recv.at[1, z], on_z[i - 1])
    yb1[y] = part[y, 0:8]
    zb1[z] = part[:, 8 + z]
    for i in range(1, 8):
        from_y = lax.rem(y + i, NY)
        arrived(yb1.at[from_y], t_recv.at[0, from_y])
    s1[...] = added(yb1).astype(BF16)
    for i in range(1, 8):
        to_z = lax.rem(z + i, NZ)
        send(s1.at[to_z], zb2.at[z], u_send.at[0, i], u_recv.at[0, z], on_z[i - 1])
    for i in range(1, 8):
        from_z = lax.rem(z + i, NZ)
        arrived(zb1.at[from_z], t_recv.at[1, from_z])
    s2[...] = added(zb1).astype(BF16)
    for i in range(1, 8):
        to_y = lax.rem(y + i, NY)
        send(s2.at[to_y], yb2.at[y], u_send.at[1, i], u_recv.at[1, y], on_y[i - 1])
    zb2[z] = s1[z]
    yb2[y] = s2[y]
    for i in range(1, 8):
        from_z = lax.rem(z + i, NZ)
        arrived(zb2.at[from_z], u_recv.at[0, from_z])
    fin[z, 0] = added(zb2).astype(BF16)
    for i in range(1, 8):
        from_y = lax.rem(y + i, NY)
        arrived(yb2.at[from_y], u_recv.at[1, from_y])
    fin[z, 1] = added(yb2).astype(BF16)
    for i in range(1, 8):
        send(fin.at[z], fin.at[z], f_send.at[i], f_recv.at[z], on_z[i - 1])
    for i in range(1, 8):
        from_z = lax.rem(z + i, NZ)
        arrived(fin.at[from_z], f_recv.at[from_z])
    send(fin, fin_sib, c_sem.at[0], c_sem.at[1], twin)
    arrived(fin_sib, c_sem.at[1])
    for half in range(2):
        mine = jnp.where(core == half, fin[...].astype(F32), fin_sib[...].astype(F32))
        wide = [
            jnp.concatenate([mine[(3 * i + j) % 8, (3 * i + j) // 8] for j in range(3)], axis=1)
            for i in range(PAD // 16)
        ]
        wide = jnp.concatenate(wide, axis=0)
        for k in range(3):
            cg_out[k, :, half * HALF : (half + 1) * HALF] = wide[k * SPAN : (k + 1) * SPAN]

    for one in sends:
        one.wait_send()


def on_device(input_rows, features, norm_gain, w_query, w_key, w_value, temper, head_grads):
    vmem = pl.BlockSpec(memory_space=pltpu.VMEM)
    dma = pltpu.SemaphoreType.DMA

    def scratch(*shape, dtype=BF16):
        return pltpu.VMEM(shape, dtype)

    fg, cg = pl.pallas_call(
        kernel,
        out_shape=(
            jax.ShapeDtypeStruct((TOK, CH), BF16),
            jax.ShapeDtypeStruct((3, SPAN, CH), F32),
        ),
        in_specs=[vmem] * 6 + [pl.BlockSpec(memory_space=pltpu.SMEM), vmem],
        out_specs=(vmem, vmem),
        scratch_shapes=[
            scratch(16, CH),
            scratch(4, HEADS, TOK, HS),
            scratch(8, QROWS, HS),
            scratch(8, QROWS, HS),
            scratch(2, QROWS, HS),
            scratch(2, TOK, HEADS * HS, dtype=F32),
            scratch(NX, NY * PAD, TOK),
            scratch(NY * PAD, 8 * TOK),
            scratch(8, QROWS, QROWS, dtype=F32),
            scratch(8, QROWS, QROWS, dtype=F32),
            scratch(8, QROWS, HS),
            scratch(8, QROWS, HS),
            scratch(NX, QROWS, HS),
            scratch(NX, QROWS, HS),
            scratch(3, QROWS, HS),
            scratch(3, QROWS, HS),
            scratch(3, QROWS, HS),
            scratch(3, QROWS, HS),
            scratch(3, QROWS, HS),
            scratch(3, HEADS, TOK, HS),
            scratch(3, TOK, HEADS * HS),
            scratch(2, TOK, HALF),
            scratch(8 * TOK, HALF),
            scratch(NY, 16, 16, 128),
            scratch(NY, 8, 16, 128),
            scratch(NZ, 8, 16, 128),
            scratch(8, 16, 128),
            scratch(8, 16, 128),
            scratch(NZ, 16, 128),
            scratch(NY, 16, 128),
            scratch(NZ, 2, 16, 128),
            scratch(NZ, 2, 16, 128),
            dma((2,)),
            dma((4, 4)), dma((4, 4)),
            dma((2, 19)), dma((2, 19)),
            dma((7,)), dma((7,)),
            dma((4,)), dma((4,)),
            dma((2, 4)), dma((2, 4)),
            dma((3,)), dma((3,)),
            dma((2, 3)), dma((2, 3)),
            dma((3, 4)), dma((3, 4)),
            dma((7,)), dma((7,)),
            dma((2, 8)), dma((2, 8)),
            dma((2, 8)), dma((2, 8)),
            dma((8,)), dma((8,)),
            dma((2,)),
        ],
        compiler_params=pltpu.CompilerParams(
            collective_id=0, has_side_effects=True, vmem_limit_bytes=56 * 1024 * 1024
        ),
    )(
        input_rows[0], features[0], norm_gain.reshape(1, CH), w_query, w_key, w_value, temper, head_grads[0],
    )
    return fg[None], cg


def solution(mesh):
    return jax.shard_map(
        on_device,
        mesh=mesh,
        in_specs=(
            P("dp", "seq", None),
            P("dp", "seq", None),
            P(),
            P(),
            P(),
            P(),
            P(),
            P("dp", "seq", None),
        ),
        out_specs=(P("dp", "seq", None), P(None, "seq", None)),
        check_vma=False,
    )
```

```python
import math

import jax
import jax.numpy as jnp
from jax import lax
from jax.experimental import pallas as pl
from jax.experimental.pallas import tpu as pltpu
from jax.sharding import PartitionSpec as P

EPSILON = 1e-06
LAST_BOTH = (((1,), (1,)), ((), ()))
FIRST_BOTH = (((0,), (0,)), ((), ()))
MESH = pl.DeviceIdType.MESH
BF16, F32 = jnp.bfloat16, jnp.float32

NX, NY, NZ = 4, 8, 8
TOK, CH, HEADS, HS = 128, 768, 4, 128
QROWS = 512
SPAN = CH // (NX * NY)
PAD = 80
HALF = CH // 2
QUARTER = CH // NX
TILES = (
    ((False, 0), (False, 1), (False, 2), (True, 0), (True, 4)),
    ((False, 3), (False, 4), (False, 5), (True, 2), (True, 6)),
    ((False, 6), (False, 7), (True, 1), (True, 3), (True, 5)),
)


def unit_rows(raw):
    inv = lax.rsqrt(jnp.mean(raw * raw, axis=-1, keepdims=True) + EPSILON)
    return raw * inv, inv


def unit_back(upstream, unit, inv):
    return inv * (upstream - unit * jnp.mean(unit * upstream, axis=-1, keepdims=True))


def kernel(
    rows_hbm, feat_ref, gain_ref, wq_hbm, wk_ref, wv_hbm, temper_ref, hg_hbm,
    fg_out, cg_out,
    rows_ref, wq_ref, wv_ref, hg_ref, prev, outgoing, keys, vals, qg, raw, wt, wbuf, e_buf, gp_buf, dv, dk, sib_v, sib_k, st_v, st_k, in_v, in_k,
    total, back, dall, fgs, fgb, tiles_y, tiles_z, yb1, zb1, s1, s2, zb2, yb2, fin, fin_sib,
    prev_sem, a_send, a_recv, k_send, k_recv, w_send, w_recv, sv_send, sv_recv, sk_send, sk_recv,
    mv_send, mv_recv, mk_send, mk_recv, b_send, b_recv, g_send, g_recv, t_send, t_recv, tz_send, tz_recv, u_send, u_recv, f_send, f_recv, c_sem, in_sem,
):
    seq, dp = lax.axis_index("seq"), lax.axis_index("dp")
    x, y = lax.div(seq, NY), lax.rem(seq, NY)
    z, core = lax.div(dp, 2), lax.rem(dp, 2)
    n_seq = NX * NY
    xr, xl, xo = lax.rem(x + 1, NX), lax.rem(x + NX - 1, NX), lax.rem(x + 2, NX)
    sib = dp + 1 - 2 * core
    part_y, head = lax.rem(y, 2), lax.div(y, 2)
    me = 2 * x + core

    def at(xx, yy):
        return xx * NY + yy

    def copy(src, dst, send, recv, where):
        return pltpu.make_async_remote_copy(
            src_ref=src, dst_ref=dst, send_sem=send, recv_sem=recv, device_id=where, device_id_type=MESH
        )

    sends = []

    def send(src, dst, send_sem, recv_sem, where):
        one = copy(src, dst, send_sem, recv_sem, where)
        one.start()
        sends.append(one)
        return one

    def arrived(dst, recv):
        copy(dst, dst, recv, recv, (seq, sib)).wait_recv()

    def rows_of(ref, start, size):
        return ref.at[pl.ds(pl.multiple_of(start, 16), size)]

    servers = [(at(x, 2 * i + core), 2 * z + 1 - lax.rem(y, 2)) for i in range(HEADS)]
    owners = [(at(x, 2 * j + 1 - core), 2 * z + part_y) for j in range(4)]
    ring_next, ring_prev = (lax.rem(seq + 1, n_seq), dp), (lax.rem(seq + n_seq - 1, n_seq), dp)
    right, left, twin, far = (at(xr, y), dp), (at(xl, y), dp), (seq, sib), (at(xo, y), dp)
    right_twin, left_twin = (at(xr, y), sib), (at(xl, y), sib)
    on_y = [(at(x, lax.rem(y + i, NY)), dp) for i in range(1, NY)]
    on_z = [(seq, lax.rem(dp + 2 * i, 2 * NZ)) for i in range(1, NZ)]

    staged = []
    for i, (src, dst) in enumerate(((wv_hbm, wv_ref), (hg_hbm, hg_ref), (wq_hbm, wq_ref), (rows_hbm, rows_ref))):
        staged.append(pltpu.make_async_copy(src, dst, in_sem.at[i]))
        staged[i].start()
    barrier = pltpu.get_barrier_semaphore()
    partners = servers + owners + [ring_next, ring_prev, right, left, twin, far, right_twin, left_twin] + on_y + on_z
    for where in partners:
        pl.semaphore_signal(barrier, inc=1, device_id=where, device_id_type=MESH)

    feats = feat_ref[...].astype(F32)
    inv_rms = lax.rsqrt(jnp.mean(feats * feats, axis=1, keepdims=True) + EPSILON)
    gain = gain_ref[...].reshape(1, CH)
    normed = (feats * inv_rms * gain).astype(BF16)
    slot = lax.div(y, 2)
    their_me = 2 * x + 1 - lax.rem(y, 2)

    def start_heads(kind, to):
        for i in range(HEADS):
            send(outgoing.at[kind, i], to, a_send.at[kind, i], a_recv.at[kind, slot], servers[i])

    def project(which, w_ref):
        raw[which] = jnp.dot(normed, w_ref[...], preferred_element_type=F32)
        for i in range(HEADS):
            outgoing[which, i] = unit_rows(raw[which, :, i * HS : (i + 1) * HS])[0].astype(BF16)

    project(0, wk_ref)
    pl.semaphore_wait(barrier, len(partners))
    slot_rows = pl.ds(pl.multiple_of(slot * TOK, TOK), TOK)
    start_heads(0, keys.at[their_me, slot_rows])
    staged[3].wait()
    send(rows_ref.at[pl.ds(2 * TOK - 16, 16)], prev, prev_sem.at[0], prev_sem.at[1], ring_next)
    staged[0].wait()
    staged[1].wait()
    values = jnp.dot(normed, wv_ref[...], preferred_element_type=F32).astype(BF16)
    for i in range(HEADS):
        outgoing[2, i] = values[:, i * HS : (i + 1) * HS]
        outgoing[3, i] = hg_ref[:, i * HS : (i + 1) * HS]
    start_heads(2, vals.at[their_me, slot_rows])
    staged[2].wait()
    project(1, wq_ref)

    def chosen(rows, columns, first_tap):
        row = lax.broadcasted_iota(jnp.int32, (rows, columns), 0)
        lane = lax.broadcasted_iota(jnp.int32, (rows, columns), 1)
        return (row == 2 * lax.rem(lane, TOK) + lax.div(lane, TOK) + first_tap - 1).astype(F32).astype(BF16)

    def w_slot(first_tap, taps, xx, cc):
        return wbuf.at[pl.ds(first_tap, taps), :, pl.ds(pl.multiple_of((2 * xx + cc) * TOK, TOK), TOK)]

    def put_windows(tap, windows):
        for i in range(NX):
            wt[i, tap] = windows[i * QUARTER : (i + 1) * QUARTER].astype(BF16)
        wbuf[tap, :, pl.ds(pl.multiple_of(me * TOK, TOK), TOK)] = wt[x, tap]

    def start_windows(group, first_tap, taps):
        some = pl.ds(first_tap, taps)
        for i, (to_x, where) in enumerate(((xl, left), (xr, right), (xo, far), (x, twin))):
            src = wt.at[to_x, some]
            send(src, w_slot(first_tap, taps, x, core), w_send.at[group, i], w_recv.at[group, i], where)

    def windows_on(group, first_tap, taps):
        for i, from_x in enumerate((xr, xl, xo)):
            piece = w_slot(first_tap, taps, from_x, core)
            arrived(piece, w_recv.at[group, i])
            send(piece, piece, w_send.at[group, 4 + i], w_recv.at[group, 4 + i], twin)

    def got_windows(group, first_tap, taps):
        for i, from_x in enumerate((x, xr, xl, xo)):
            arrived(w_slot(first_tap, taps, from_x, 1 - core), w_recv.at[group, 3 + i])

    windows = lax.dot_general(rows_ref[...], chosen(2 * TOK, 2 * TOK, 1), FIRST_BOTH, preferred_element_type=F32)
    put_windows(1, windows[:, 0:TOK])
    put_windows(2, windows[:, TOK:])
    start_windows(0, 1, 2)
    start_heads(1, qg.at[0, slot_rows])
    arrived(prev, prev_sem.at[1])
    row = lax.broadcasted_iota(jnp.int32, (16, TOK), 0)
    lane = lax.broadcasted_iota(jnp.int32, (16, TOK), 1)
    first = ((row == 15) & (lane == 0) & (seq > 0)).astype(F32).astype(BF16)
    windows = lax.dot_general(rows_ref[...], chosen(2 * TOK, TOK, 0), FIRST_BOTH, preferred_element_type=F32)
    put_windows(0, windows + lax.dot_general(prev[...], first, FIRST_BOTH, preferred_element_type=F32))

    def chunk(ref, block, i):
        j = lax.rem(slot + (0, 1, 3, 2)[i], 4)
        return ref.at[block, pl.ds(pl.multiple_of(j * TOK, TOK), TOK)], j

    from_left, from_right, from_far = 2 * xl + core, 2 * xr + core, 2 * xo + core
    twin_me, twin_left, twin_right, twin_far = me + 1 - 2 * core, 2 * xl + 1 - core, 2 * xr + 1 - core, 2 * xo + 1 - core
    both = (keys, vals)

    def ring_own(t, i):
        mine, j = chunk(both[t], me, i)
        arrived(mine, a_recv.at[2 * t, j])
        for k, where in enumerate((right, left, twin)):
            send(mine, mine, k_send.at[t, 3 * i + k], k_recv.at[t, (0, 4, 12)[k] + i], where)

    def ring_on(t):
        for i, block, first_slot, onward in (
            (0, from_left, 0, right), (1, from_left, 0, right), (0, from_right, 4, None), (1, from_right, 4, None),
            (2, from_right, 4, left), (3, from_right, 4, left), (2, from_left, 0, None), (3, from_left, 0, None),
        ):
            piece, _ = chunk(both[t], block, i)
            arrived(piece, k_recv.at[t, first_slot + i])
            if onward is not None:
                send(piece, piece, k_send.at[t, 12 + i], k_recv.at[t, 8 + i], onward)
        for k, block in enumerate((from_left, from_right)):
            send(both[t].at[block], both[t].at[block], k_send.at[t, 16 + k], k_recv.at[t, 16 + k], twin)

    def ring_far(t):
        for i in range(4):
            arrived(chunk(both[t], from_far, i)[0], k_recv.at[t, 8 + i])
        send(both[t].at[from_far], both[t].at[from_far], k_send.at[t, 18], k_recv.at[t, 18], twin)

    def got_twin(t):
        for i in range(4):
            arrived(chunk(both[t], twin_me, i)[0], k_recv.at[t, 12 + i])

    def got_from_twin(t, k):
        arrived(both[t].at[(twin_left, twin_right, twin_far)[k]], k_recv.at[t, 16 + k])

    for i in range(4):
        ring_own(0, i)
    start_heads(3, qg.at[1, slot_rows])
    for i in range(4):
        ring_own(1, i)
    ring_on(0)

    for j in range(4):
        arrived(qg.at[0, pl.ds(j * TOK, TOK)], a_recv.at[1, j])
    factor = temper_ref[head] * (1.0 / math.sqrt(HS))

    def score_pass(block, exp_sum):
        scores = lax.dot_general(keys[block], qg[0], LAST_BOTH, preferred_element_type=F32)
        expo = jnp.exp2(scores * (factor * math.log2(math.e)))
        e_buf[block] = expo
        return exp_sum + jnp.sum(expo, axis=0, keepdims=True)

    exp_sum = score_pass(me, jnp.zeros((1, QROWS), F32))
    got_twin(0)
    exp_sum = score_pass(twin_me, exp_sum)
    ring_on(1)
    exp_sum = score_pass(from_left, exp_sum)
    exp_sum = score_pass(from_right, exp_sum)
    ring_far(0)
    got_from_twin(0, 0)
    exp_sum = score_pass(twin_left, exp_sum)
    got_from_twin(0, 1)
    exp_sum = score_pass(twin_right, exp_sum)
    exp_sum = score_pass(from_far, exp_sum)
    got_from_twin(0, 2)
    exp_sum = score_pass(twin_far, exp_sum)
    inv_sum = 1.0 / exp_sum

    for j in range(4):
        arrived(qg.at[1, pl.ds(j * TOK, TOK)], a_recv.at[3, j])
    order = (xo, xr, xl, x)
    to = (far, right, left)

    def value_grad(block):
        prob = (e_buf[block] * inv_sum).astype(BF16)
        dv[block] = jnp.dot(prob, qg[1], preferred_element_type=F32).astype(BF16)

    def prob_grad(block, dot_sum):
        grad_prob = lax.dot_general(vals[block], qg[1], LAST_BOTH, preferred_element_type=F32)
        gp_buf[block] = grad_prob
        return dot_sum + jnp.sum(e_buf[block] * grad_prob, axis=0, keepdims=True)

    def pass_values(i):
        arrived(sib_v.at[i], sv_recv.at[i])
        st_v[i] = (dv[2 * order[i] + core].astype(F32) + sib_v[i].astype(F32)).astype(BF16)
        send(st_v.at[i], in_v.at[i], mv_send.at[i], mv_recv.at[i], to[i])

    dot_sum = jnp.zeros((1, QROWS), F32)
    for i in range(NX):
        block = 2 * order[i] + 1 - core
        value_grad(block)
        send(dv.at[block], sib_v.at[i], sv_send.at[i], sv_recv.at[i], twin)
        value_grad(2 * order[i] + core)
        if i > 0:
            pass_values(i - 1)
        if i == 0:
            dot_sum = prob_grad(me, dot_sum)
            got_twin(1)
            dot_sum = prob_grad(twin_me, dot_sum)
        elif i == 1:
            dot_sum = prob_grad(from_left, dot_sum)
            dot_sum = prob_grad(from_right, dot_sum)
            ring_far(1)
        elif i == 2:
            for k, other in enumerate((twin_left, twin_right)):
                got_from_twin(1, k)
                dot_sum = prob_grad(other, dot_sum)
        else:
            dot_sum = prob_grad(from_far, dot_sum)
            got_from_twin(1, 2)
            dot_sum = prob_grad(twin_far, dot_sum)

    windows_on(0, 1, 2)

    grad_dot = dot_sum * inv_sum
    inv_factor = inv_sum * factor
    half_rows = QROWS // 2

    def key_grad(block, half, grad_query):
        low = half * half_rows
        high = low + half_rows
        grad_score = (e_buf[block, low:high] * inv_factor * (gp_buf[block, low:high] - grad_dot)).astype(BF16)
        dk[block, low:high] = jnp.dot(grad_score, qg[0], preferred_element_type=F32).astype(BF16)
        keys_t = jnp.transpose(keys[block, low:high])
        return grad_query + jnp.dot(keys_t, grad_score, preferred_element_type=F32)

    def half_of(ref, i, half):
        return ref.at[i, pl.ds(half * half_rows, half_rows)]

    def pass_keys(half, i):
        low = half * half_rows
        high = low + half_rows
        arrived(half_of(sib_k, i, half), sk_recv.at[half, i])
        summed = dk[2 * order[i] + core, low:high].astype(F32) + sib_k[i, low:high].astype(F32)
        if i < 3:
            st_k[i, low:high] = summed.astype(BF16)
            send(half_of(st_k, i, half), half_of(in_k, i, half), mk_send.at[half, i], mk_recv.at[half, i], to[i])
        return summed

    def start_back(kind, j):
        src = total.at[kind, pl.ds(j * TOK, TOK)]
        send(src, back.at[kind, head], b_send.at[kind, j], b_recv.at[kind, head], owners[j])

    def finish_values():
        arrived(sib_v.at[3], sv_recv.at[3])
        summed = dv[me].astype(F32) + sib_v[3].astype(F32)
        for i in range(3):
            arrived(in_v.at[i], mv_recv.at[i])
            summed += in_v[i].astype(F32)
        total[2] = summed.astype(BF16)
        for j in range(4):
            start_back(2, j)

    grad_query = jnp.zeros((HS, QROWS), F32)
    pending = None
    for half in range(2):
        for i in range(NX):
            block = 2 * order[i] + 1 - core
            grad_query = key_grad(block, half, grad_query)
            send(half_of(dk, block, half), half_of(sib_k, i, half), sk_send.at[half, i], sk_recv.at[half, i], twin)
            grad_query = key_grad(2 * order[i] + core, half, grad_query)
            if pending is not None and pending[1] < 3:
                pass_keys(*pending)
            pending = (half, i)
            if pending == (1, 2):
                finish_values()
    total[0] = jnp.transpose(grad_query).astype(BF16)

    for j in range(4):
        start_back(0, j)
    for half in range(2):
        low = half * half_rows
        high = low + half_rows
        summed = pass_keys(half, 3)
        for i in range(3):
            arrived(half_of(in_k, i, half), mk_recv.at[half, i])
            summed += in_k[i, low:high].astype(F32)
        total[1, low:high] = summed.astype(BF16)
        for j in range(2 * half, 2 * half + 2):
            start_back(1, j)

    start_windows(1, 0, 1)

    def put_raw_grad(which, i, upstream_grad):
        unit, inv = unit_rows(raw[1 - which, :, i * HS : (i + 1) * HS])
        dall[which, :, i * HS : (i + 1) * HS] = unit_back(upstream_grad.astype(F32), unit, inv).astype(BF16)

    for i in range(HEADS):
        arrived(back.at[0, i], b_recv.at[0, i])
        put_raw_grad(0, i, back[0, i])
    grad_normed = lax.dot_general(dall[0], wq_ref[...], LAST_BOTH, preferred_element_type=F32)
    for i in range(HEADS):
        arrived(back.at[2, i], b_recv.at[2, i])
        dall[2, :, i * HS : (i + 1) * HS] = back[2, i]
    grad_normed += lax.dot_general(dall[2], wv_ref[...], LAST_BOTH, preferred_element_type=F32)
    for i in range(HEADS):
        arrived(back.at[1, i], b_recv.at[1, i])
        put_raw_grad(1, i, back[1, i])
    grad_normed += lax.dot_general(dall[1], wk_ref[...], LAST_BOTH, preferred_element_type=F32)
    gained = grad_normed * gain
    unit_feats = feats * inv_rms
    feature_grad = inv_rms * (gained - unit_feats * jnp.mean(unit_feats * gained, axis=1, keepdims=True))
    feature_grad = feature_grad.astype(BF16)
    fg_out[...] = feature_grad
    for i in range(2):
        for k in range(3):
            fgs[i, k] = feature_grad[:, i * HALF + k * 128 : i * HALF + (k + 1) * 128]

    def g_slot(k, xx, cc):
        return fgb.at[k, pl.ds(pl.multiple_of((2 * xx + cc) * TOK, TOK), TOK)]

    for k in range(3):
        for i, (where, cc, slot_at) in enumerate(
            (
                (right, core, core),
                (left, core, 2 + core),
                (right_twin, 1 - core, core),
                (left_twin, 1 - core, 2 + core),
                (twin, 1 - core, 6),
            )
        ):
            send(fgs.at[cc, k], g_slot(k, x, core), g_send.at[k, i], g_recv.at[k, slot_at], where)
        fgb[k, pl.ds(pl.multiple_of(me * TOK, TOK), TOK)] = fgs[core, k]
    windows_on(1, 0, 1)

    def gather_on(k):
        arrived(g_slot(k, xl, 0), g_recv.at[k, 0])
        send(g_slot(k, xl, 0), g_slot(k, xl, 0), g_send.at[k, 5], g_recv.at[k, 4], right)
        arrived(g_slot(k, xr, 1), g_recv.at[k, 3])
        send(g_slot(k, xr, 1), g_slot(k, xr, 1), g_send.at[k, 6], g_recv.at[k, 5], left)

    def sum_chunk(k):
        arrived(g_slot(k, xl, 1), g_recv.at[k, 1])
        arrived(g_slot(k, xr, 0), g_recv.at[k, 2])
        arrived(g_slot(k, x, 1 - core), g_recv.at[k, 6])
        arrived(g_slot(k, xo, 0), g_recv.at[k, 4])
        arrived(g_slot(k, xo, 1), g_recv.at[k, 5])
        terms = jnp.dot(wbuf[...].reshape(3 * QUARTER, 8 * TOK), fgb[k], preferred_element_type=F32) * (1.0 / (2 * NZ))
        for b in range(NY):
            taps = [terms[i * QUARTER + b * SPAN : i * QUARTER + (b + 1) * SPAN] for i in range(3)]
            rows = jnp.concatenate(taps + [jnp.zeros((PAD - 3 * SPAN, 128), F32)], axis=0).astype(BF16)
            for i, (by_z, at_tile) in enumerate(TILES[k]):
                tile = rows[16 * i : 16 * (i + 1)]
                if by_z:
                    tiles_z[at_tile, b] = tile
                else:
                    tiles_y[b, at_tile] = tile
        of_y = [at_tile for by_z, at_tile in TILES[k] if not by_z]
        some = pl.ds(of_y[0], len(of_y))
        for i in range(1, NY):
            to_y = lax.rem(y + i, NY)
            send(tiles_y.at[to_y, some], yb1.at[y, some], t_send.at[k, i], t_recv.at[k, y], on_y[i - 1])
        yb1[y, some] = tiles_y[y, some]
        for by_z, at_tile in TILES[k]:
            if by_z:

                @pl.when(z != at_tile)
                def _():
                    to_owner(at_tile).start()

                @pl.when(z == at_tile)
                def _():
                    zb1[z] = tiles_z[at_tile]

    def to_owner(at_tile):
        return copy(tiles_z.at[at_tile], zb1.at[z], tz_send.at[at_tile], tz_recv.at[z], (seq, 2 * at_tile + core))

    def added(ref):
        out = ref[0].astype(F32)
        for i in range(1, 8):
            out += ref[i].astype(F32)
        return out

    @pl.when(z == NZ - 1)
    def _():
        zb1[...] = jnp.zeros_like(zb1)

    gather_on(0)
    gather_on(1)
    got_windows(0, 1, 2)
    got_windows(1, 0, 1)
    sum_chunk(0)
    gather_on(2)
    sum_chunk(1)
    sum_chunk(2)
    for i in range(1, NY):
        from_y = lax.rem(y + i, NY)
        for k in range(3):
            of_y = [at_tile for by_z, at_tile in TILES[k] if not by_z]
            arrived(yb1.at[from_y, pl.ds(of_y[0], len(of_y))], t_recv.at[k, from_y])
    s1[...] = added(yb1).astype(BF16)
    for i in range(1, 8):
        to_z = lax.rem(z + i, NZ)
        send(s1.at[to_z], zb2.at[z], u_send.at[0, i], u_recv.at[0, z], on_z[i - 1])

    @pl.when(z < NZ - 1)
    def _():
        for i in range(1, 8):
            from_z = lax.rem(z + i, NZ)
            arrived(zb1.at[from_z], tz_recv.at[from_z])

    s2[...] = added(zb1).astype(BF16)
    for i in range(1, 8):
        to_y = lax.rem(y + i, NY)
        send(s2.at[to_y], yb2.at[y], u_send.at[1, i], u_recv.at[1, y], on_y[i - 1])
    zb2[z] = s1[z]
    yb2[y] = s2[y]
    for i in range(1, 8):
        from_z = lax.rem(z + i, NZ)
        arrived(zb2.at[from_z], u_recv.at[0, from_z])
    fin[z, 0] = added(zb2).astype(BF16)
    for i in range(1, 8):
        from_y = lax.rem(y + i, NY)
        arrived(yb2.at[from_y], u_recv.at[1, from_y])
    fin[z, 1] = added(yb2).astype(BF16)
    for i in range(1, 8):
        send(fin.at[z], fin.at[z], f_send.at[i], f_recv.at[z], on_z[i - 1])
    for i in range(1, 8):
        from_z = lax.rem(z + i, NZ)
        arrived(fin.at[from_z], f_recv.at[from_z])
    send(fin, fin_sib, c_sem.at[0], c_sem.at[1], twin)
    arrived(fin_sib, c_sem.at[1])
    for half in range(2):
        mine = jnp.where(core == half, fin[...].astype(F32), fin_sib[...].astype(F32))
        wide = []
        for i in range(PAD // 16):
            row = [TILES[k][i] for k in range(3)]
            wide.append(jnp.concatenate([mine[at_tile, int(by_z)] for by_z, at_tile in row], axis=1))
        wide = jnp.concatenate(wide, axis=0)
        for k in range(3):
            cg_out[k, :, half * HALF : (half + 1) * HALF] = wide[k * SPAN : (k + 1) * SPAN]

    for one in sends:
        one.wait_send()
    for at_tile in range(NZ - 1):

        @pl.when(z != at_tile)
        def _():
            to_owner(at_tile).wait_send()


def on_device(input_rows, features, norm_gain, w_query, w_key, w_value, temper, head_grads):
    vmem, hbm = pl.BlockSpec(memory_space=pltpu.VMEM), pl.BlockSpec(memory_space=pl.ANY)
    dma = pltpu.SemaphoreType.DMA

    def scratch(*shape, dtype=BF16):
        return pltpu.VMEM(shape, dtype)

    fg, cg = pl.pallas_call(
        kernel,
        out_shape=(
            jax.ShapeDtypeStruct((TOK, CH), BF16),
            jax.ShapeDtypeStruct((3, SPAN, CH), F32),
        ),
        in_specs=[hbm, vmem, vmem, hbm, vmem, hbm, pl.BlockSpec(memory_space=pltpu.SMEM), hbm],
        out_specs=(vmem, vmem),
        scratch_shapes=[
            scratch(2 * TOK, CH),
            scratch(CH, HEADS * HS),
            scratch(CH, HEADS * HS),
            scratch(TOK, HEADS * HS),
            scratch(16, CH),
            scratch(4, HEADS, TOK, HS),
            scratch(8, QROWS, HS),
            scratch(8, QROWS, HS),
            scratch(2, QROWS, HS),
            scratch(2, TOK, HEADS * HS, dtype=F32),
            scratch(NX, 3, QUARTER, TOK),
            scratch(3, QUARTER, 8 * TOK),
            scratch(8, QROWS, QROWS, dtype=F32),
            scratch(8, QROWS, QROWS, dtype=F32),
            scratch(8, QROWS, HS),
            scratch(8, QROWS, HS),
            scratch(NX, QROWS, HS),
            scratch(NX, QROWS, HS),
            scratch(3, QROWS, HS),
            scratch(3, QROWS, HS),
            scratch(3, QROWS, HS),
            scratch(3, QROWS, HS),
            scratch(3, QROWS, HS),
            scratch(3, HEADS, TOK, HS),
            scratch(3, TOK, HEADS * HS),
            scratch(2, 3, TOK, 128),
            scratch(3, 8 * TOK, 128),
            scratch(NY, 8, 16, 128),
            scratch(NZ, NY, 16, 128),
            scratch(NY, 8, 16, 128),
            scratch(NZ, 8, 16, 128),
            scratch(8, 16, 128),
            scratch(8, 16, 128),
            scratch(NZ, 16, 128),
            scratch(NY, 16, 128),
            scratch(NZ, 2, 16, 128),
            scratch(NZ, 2, 16, 128),
            dma((2,)),
            dma((4, 4)), dma((4, 4)),
            dma((2, 19)), dma((2, 19)),
            dma((2, 7)), dma((2, 7)),
            dma((4,)), dma((4,)),
            dma((2, 4)), dma((2, 4)),
            dma((3,)), dma((3,)),
            dma((2, 3)), dma((2, 3)),
            dma((3, 4)), dma((3, 4)),
            dma((3, 7)), dma((3, 7)),
            dma((3, 8)), dma((3, 8)),
            dma((8,)), dma((8,)),
            dma((2, 8)), dma((2, 8)),
            dma((8,)), dma((8,)),
            dma((2,)),
            dma((4,)),
        ],
        compiler_params=pltpu.CompilerParams(
            collective_id=0, has_side_effects=True, vmem_limit_bytes=56 * 1024 * 1024
        ),
    )(
        input_rows[0], features[0], norm_gain, w_query, w_key, w_value, temper, head_grads[0],
    )
    return fg[None], cg


def solution(mesh):
    return jax.shard_map(
        on_device,
        mesh=mesh,
        in_specs=(
            P("dp", "seq", None),
            P("dp", "seq", None),
            P(),
            P(),
            P(),
            P(),
            P(),
            P("dp", "seq", None),
        ),
        out_specs=(P("dp", "seq", None), P(None, "seq", None)),
        check_vma=False,
    )
```

```python
import math

import jax
import jax.numpy as jnp
from jax import lax
from jax.experimental import pallas as pl
from jax.experimental.pallas import tpu as pltpu
from jax.sharding import PartitionSpec as P

EPSILON = 1e-06
LAST_BOTH = (((1,), (1,)), ((), ()))
FIRST_BOTH = (((0,), (0,)), ((), ()))
MESH = pl.DeviceIdType.MESH
BF16, F32 = jnp.bfloat16, jnp.float32

NX, NY, NZ = 4, 8, 8
TOK, CH, HEADS, HS = 128, 768, 4, 128
QROWS = 512
SPAN = CH // (NX * NY)
PAD = 80
HALF = CH // 2
QUARTER = CH // NX
TILES = (
    ((False, 0), (False, 1), (True, 0), (True, 3), (True, 6)),
    ((False, 2), (False, 3), (False, 4), (True, 1), (True, 4)),
    ((False, 5), (False, 6), (False, 7), (True, 2), (True, 5)),
)


def unit_rows(raw):
    inv = lax.rsqrt(jnp.mean(raw * raw, axis=-1, keepdims=True) + EPSILON)
    return raw * inv, inv


def unit_back(upstream, unit, inv):
    return inv * (upstream - unit * jnp.mean(unit * upstream, axis=-1, keepdims=True))


def kernel(
    rows_hbm, feat_hbm, gain_hbm, wq_hbm, wk_hbm, wv_hbm, temper_hbm, hg_hbm,
    fg_out, cg_out,
    rows_ref, feat_ref, gain_ref, wq_ref, wk_ref, wv_ref, temper_ref, hg_ref, prev, outgoing, keys, vals, qg, raw, wt, wbuf, e_buf, gp_buf, dv, dk, sib_v, sib_k, st_v, st_k, in_v, in_k,
    total, back, dall, fgs, fgb, tiles_y, tiles_z, yb1, zb1, s1, s2, zb2, yb2, fin, fin_sib,
    prev_sem, a_send, a_recv, k_send, k_recv, w_send, w_recv, sv_send, sv_recv, sk_send, sk_recv,
    mv_send, mv_recv, mk_send, mk_recv, b_send, b_recv, g_send, g_recv, t_send, t_recv, tz_send, tz_recv, u_send, u_recv, f_send, f_recv, c_sem, in_sem,
):
    seq, dp = lax.axis_index("seq"), lax.axis_index("dp")
    x, y = lax.div(seq, NY), lax.rem(seq, NY)
    z, core = lax.div(dp, 2), lax.rem(dp, 2)
    n_seq = NX * NY
    xr, xl, xo = lax.rem(x + 1, NX), lax.rem(x + NX - 1, NX), lax.rem(x + 2, NX)
    sib = dp + 1 - 2 * core
    part_y, head = lax.rem(y, 2), lax.div(y, 2)
    me = 2 * x + core

    def at(xx, yy):
        return xx * NY + yy

    def copy(src, dst, send, recv, where):
        return pltpu.make_async_remote_copy(
            src_ref=src, dst_ref=dst, send_sem=send, recv_sem=recv, device_id=where, device_id_type=MESH
        )

    sends = []

    def send(src, dst, send_sem, recv_sem, where):
        one = copy(src, dst, send_sem, recv_sem, where)
        one.start()
        sends.append(one)
        return one

    def arrived(dst, recv):
        copy(dst, dst, recv, recv, (seq, sib)).wait_recv()

    def rows_of(ref, start, size):
        return ref.at[pl.ds(pl.multiple_of(start, 16), size)]

    servers = [(at(x, 2 * i + core), 2 * z + 1 - lax.rem(y, 2)) for i in range(HEADS)]
    owners = [(at(x, 2 * j + 1 - core), 2 * z + part_y) for j in range(4)]
    ring_next, ring_prev = (lax.rem(seq + 1, n_seq), dp), (lax.rem(seq + n_seq - 1, n_seq), dp)
    right, left, twin, far = (at(xr, y), dp), (at(xl, y), dp), (seq, sib), (at(xo, y), dp)
    right_twin, left_twin, far_twin = (at(xr, y), sib), (at(xl, y), sib), (at(xo, y), sib)
    on_y = [(at(x, lax.rem(y + i, NY)), dp) for i in range(1, NY)]
    on_z = [(seq, lax.rem(dp + 2 * i, 2 * NZ)) for i in range(1, NZ)]

    barrier = pltpu.get_barrier_semaphore()
    partners = servers + owners + [ring_next, ring_prev, right, left, twin, far, right_twin, left_twin, far_twin] + on_y + on_z
    for where in partners:
        pl.semaphore_signal(barrier, inc=1, device_id=where, device_id_type=MESH)

    staged = []
    for i, (src, dst) in enumerate(
        (
            (feat_hbm, feat_ref), (gain_hbm, gain_ref), (wk_hbm, wk_ref), (temper_hbm, temper_ref),
            (wv_hbm, wv_ref), (hg_hbm, hg_ref), (rows_hbm, rows_ref), (wq_hbm, wq_ref),
        )
    ):
        staged.append(pltpu.make_async_copy(src, dst, in_sem.at[i]))
        staged[i].start()

    for one in staged[:4]:
        one.wait()
    feats = feat_ref[...].astype(F32)
    inv_rms = lax.rsqrt(jnp.mean(feats * feats, axis=1, keepdims=True) + EPSILON)
    gain = gain_ref[...].reshape(1, CH)
    normed = (feats * inv_rms * gain).astype(BF16)
    slot = lax.div(y, 2)
    their_me = 2 * x + 1 - lax.rem(y, 2)

    def start_heads(kind, to):
        started = []
        for i in range(HEADS):
            started.append(copy(outgoing.at[kind, i], to, a_send.at[kind, i], a_recv.at[kind, slot], servers[i]))
            started[i].start()
        return started

    def wait_heads(started):
        for one in started:
            one.wait_send()

    def project(which, w_ref):
        raw[which] = jnp.dot(normed, w_ref[...], preferred_element_type=F32)
        for i in range(HEADS):
            outgoing[which, i] = unit_rows(raw[which, :, i * HS : (i + 1) * HS])[0].astype(BF16)

    project(0, wk_ref)
    pl.semaphore_wait(barrier, len(partners))
    slot_rows = pl.ds(pl.multiple_of(slot * TOK, TOK), TOK)
    sent = start_heads(0, keys.at[their_me, slot_rows])
    staged[6].wait()
    send(rows_ref.at[pl.ds(2 * TOK - 16, 16)], prev, prev_sem.at[0], prev_sem.at[1], ring_next)
    staged[4].wait()
    staged[5].wait()
    values = jnp.dot(normed, wv_ref[...], preferred_element_type=F32).astype(BF16)
    for i in range(HEADS):
        outgoing[2, i] = values[:, i * HS : (i + 1) * HS]
        outgoing[3, i] = hg_ref[:, i * HS : (i + 1) * HS]

    def chosen(rows, columns, first_tap):
        row = lax.broadcasted_iota(jnp.int32, (rows, columns), 0)
        lane = lax.broadcasted_iota(jnp.int32, (rows, columns), 1)
        return (row == 2 * lax.rem(lane, TOK) + lax.div(lane, TOK) + first_tap - 1).astype(F32).astype(BF16)

    def w_slot(first_tap, taps, xx, cc):
        return wbuf.at[pl.ds(first_tap, taps), :, pl.ds(pl.multiple_of((2 * xx + cc) * TOK, TOK), TOK)]

    def put_windows(tap, windows):
        for i in range(NX):
            wt[i, tap] = windows[i * QUARTER : (i + 1) * QUARTER].astype(BF16)
        wbuf[tap, :, pl.ds(pl.multiple_of(me * TOK, TOK), TOK)] = wt[x, tap]

    def start_windows(group, first_tap, taps):
        some = pl.ds(first_tap, taps)
        for i, (to_x, where) in enumerate(((xl, left), (xr, right), (xo, far), (x, twin))):
            src = wt.at[to_x, some]
            send(src, w_slot(first_tap, taps, x, core), w_send.at[group, i], w_recv.at[group, i], where)

    def windows_on(group, first_tap, taps):
        for i, from_x in enumerate((xr, xl, xo)):
            piece = w_slot(first_tap, taps, from_x, core)
            arrived(piece, w_recv.at[group, i])
            send(piece, piece, w_send.at[group, 4 + i], w_recv.at[group, 4 + i], twin)

    def got_windows(group, first_tap, taps):
        for i, from_x in enumerate((x, xr, xl, xo)):
            arrived(w_slot(first_tap, taps, from_x, 1 - core), w_recv.at[group, 3 + i])

    windows = lax.dot_general(rows_ref[...], chosen(2 * TOK, 2 * TOK, 1), FIRST_BOTH, preferred_element_type=F32)
    put_windows(1, windows[:, 0:TOK])
    put_windows(2, windows[:, TOK:])
    start_windows(0, 1, 2)
    wait_heads(sent)
    sends += start_heads(2, vals.at[their_me, slot_rows])
    staged[7].wait()
    project(1, wq_ref)
    arrived(prev, prev_sem.at[1])
    row = lax.broadcasted_iota(jnp.int32, (16, TOK), 0)
    lane = lax.broadcasted_iota(jnp.int32, (16, TOK), 1)
    first = ((row == 15) & (lane == 0) & (seq > 0)).astype(F32).astype(BF16)
    windows = lax.dot_general(rows_ref[...], chosen(2 * TOK, TOK, 0), FIRST_BOTH, preferred_element_type=F32)
    put_windows(0, windows + lax.dot_general(prev[...], first, FIRST_BOTH, preferred_element_type=F32))

    def chunk(ref, block, i):
        j = lax.rem(slot + (0, 1, 3, 2)[i], 4)
        return ref.at[block, pl.ds(pl.multiple_of(j * TOK, TOK), TOK)], j

    from_left, from_right, from_far = 2 * xl + core, 2 * xr + core, 2 * xo + core
    twin_me, twin_left, twin_right, twin_far = me + 1 - 2 * core, 2 * xl + 1 - core, 2 * xr + 1 - core, 2 * xo + 1 - core
    both = (keys, vals)

    def ring_own(t, i):
        mine, j = chunk(both[t], me, i)
        arrived(mine, a_recv.at[2 * t, j])
        for k, where in enumerate((right, left, twin)):
            send(mine, mine, k_send.at[t, 3 * i + k], k_recv.at[t, (0, 4, 12)[k] + i], where)

    def ring_on(t):
        for i, block, first_slot, onward in (
            (0, from_left, 0, right), (1, from_left, 0, right), (0, from_right, 4, None), (1, from_right, 4, None),
            (2, from_right, 4, left), (3, from_right, 4, left), (2, from_left, 0, None), (3, from_left, 0, None),
        ):
            piece, _ = chunk(both[t], block, i)
            arrived(piece, k_recv.at[t, first_slot + i])
            if onward is not None:
                send(piece, piece, k_send.at[t, 12 + i], k_recv.at[t, 8 + i], onward)
        for k, block in enumerate((from_left, from_right)):
            send(both[t].at[block], both[t].at[block], k_send.at[t, 16 + k], k_recv.at[t, 16 + k], twin)

    def ring_far(t):
        for i in range(4):
            arrived(chunk(both[t], from_far, i)[0], k_recv.at[t, 8 + i])
        send(both[t].at[from_far], both[t].at[from_far], k_send.at[t, 18], k_recv.at[t, 18], twin)

    def got_twin(t):
        for i in range(4):
            arrived(chunk(both[t], twin_me, i)[0], k_recv.at[t, 12 + i])

    def got_from_twin(t, k):
        arrived(both[t].at[(twin_left, twin_right, twin_far)[k]], k_recv.at[t, 16 + k])

    ring_own(0, 0)
    ring_own(0, 1)
    sends += start_heads(1, qg.at[0, slot_rows])
    ring_own(0, 2)
    ring_own(0, 3)
    ring_own(1, 0)
    ring_own(1, 1)
    sends += start_heads(3, qg.at[1, slot_rows])
    ring_own(1, 2)
    ring_own(1, 3)
    ring_on(0)

    for j in range(4):
        arrived(qg.at[0, pl.ds(j * TOK, TOK)], a_recv.at[1, j])
    factor = temper_ref[head] * (1.0 / math.sqrt(HS))

    def score_pass(block, exp_sum):
        scores = lax.dot_general(keys[block], qg[0], LAST_BOTH, preferred_element_type=F32)
        expo = jnp.exp2(scores * (factor * math.log2(math.e)))
        e_buf[block] = expo
        return exp_sum + jnp.sum(expo, axis=0, keepdims=True)

    exp_sum = score_pass(me, jnp.zeros((1, QROWS), F32))
    got_twin(0)
    exp_sum = score_pass(twin_me, exp_sum)
    ring_on(1)
    exp_sum = score_pass(from_left, exp_sum)
    exp_sum = score_pass(from_right, exp_sum)
    ring_far(0)
    got_from_twin(0, 0)
    exp_sum = score_pass(twin_left, exp_sum)
    got_from_twin(0, 1)
    exp_sum = score_pass(twin_right, exp_sum)
    exp_sum = score_pass(from_far, exp_sum)
    got_from_twin(0, 2)
    exp_sum = score_pass(twin_far, exp_sum)
    inv_sum = 1.0 / exp_sum

    for j in range(4):
        arrived(qg.at[1, pl.ds(j * TOK, TOK)], a_recv.at[3, j])
    order = (xo, xr, xl, x)
    to = (far, right, left)

    def value_grad(block):
        prob = (e_buf[block] * inv_sum).astype(BF16)
        dv[block] = jnp.dot(prob, qg[1], preferred_element_type=F32).astype(BF16)

    def prob_grad(block, dot_sum):
        grad_prob = lax.dot_general(vals[block], qg[1], LAST_BOTH, preferred_element_type=F32)
        gp_buf[block] = grad_prob
        return dot_sum + jnp.sum(e_buf[block] * grad_prob, axis=0, keepdims=True)

    def pass_values(i):
        arrived(sib_v.at[i], sv_recv.at[i])
        st_v[i] = (dv[2 * order[i] + core].astype(F32) + sib_v[i].astype(F32)).astype(BF16)
        send(st_v.at[i], in_v.at[i], mv_send.at[i], mv_recv.at[i], to[i])

    dot_sum = jnp.zeros((1, QROWS), F32)
    for i in range(NX):
        block = 2 * order[i] + 1 - core
        value_grad(block)
        send(dv.at[block], sib_v.at[i], sv_send.at[i], sv_recv.at[i], twin)
        value_grad(2 * order[i] + core)
        if i > 1:
            pass_values(i - 2)
    dot_sum = prob_grad(me, dot_sum)
    pass_values(2)
    got_twin(1)
    dot_sum = prob_grad(twin_me, dot_sum)
    dot_sum = prob_grad(from_left, dot_sum)
    dot_sum = prob_grad(from_right, dot_sum)
    ring_far(1)
    for k, other in enumerate((twin_left, twin_right)):
        got_from_twin(1, k)
        dot_sum = prob_grad(other, dot_sum)
    dot_sum = prob_grad(from_far, dot_sum)
    got_from_twin(1, 2)
    dot_sum = prob_grad(twin_far, dot_sum)
    windows_on(0, 1, 2)

    grad_dot = dot_sum * inv_sum
    inv_factor = inv_sum * factor
    half_rows = QROWS // 2

    def key_grad(block, half, grad_query):
        low = half * half_rows
        high = low + half_rows
        grad_score = (e_buf[block, low:high] * inv_factor * (gp_buf[block, low:high] - grad_dot)).astype(BF16)
        dk[block, low:high] = jnp.dot(grad_score, qg[0], preferred_element_type=F32).astype(BF16)
        keys_t = jnp.transpose(keys[block, low:high])
        return grad_query + jnp.dot(keys_t, grad_score, preferred_element_type=F32)

    def half_of(ref, i, half):
        return ref.at[i, pl.ds(half * half_rows, half_rows)]

    def pass_keys(half, i):
        low = half * half_rows
        high = low + half_rows
        arrived(half_of(sib_k, i, half), sk_recv.at[half, i])
        summed = dk[2 * order[i] + core, low:high].astype(F32) + sib_k[i, low:high].astype(F32)
        if i < 3:
            st_k[i, low:high] = summed.astype(BF16)
            send(half_of(st_k, i, half), half_of(in_k, i, half), mk_send.at[half, i], mk_recv.at[half, i], to[i])
        return summed

    def start_back(kind, j):
        src = total.at[kind, pl.ds(j * TOK, TOK)]
        send(src, back.at[kind, head], b_send.at[kind, j], b_recv.at[kind, head], owners[j])

    def finish_values():
        arrived(sib_v.at[3], sv_recv.at[3])
        summed = dv[me].astype(F32) + sib_v[3].astype(F32)
        for i in range(3):
            arrived(in_v.at[i], mv_recv.at[i])
            summed += in_v[i].astype(F32)
        total[2] = summed.astype(BF16)
        for j in range(4):
            start_back(2, j)

    grad_query = jnp.zeros((HS, QROWS), F32)
    pending = None
    for half in range(2):
        for i in range(NX):
            block = 2 * order[i] + 1 - core
            grad_query = key_grad(block, half, grad_query)
            send(half_of(dk, block, half), half_of(sib_k, i, half), sk_send.at[half, i], sk_recv.at[half, i], twin)
            grad_query = key_grad(2 * order[i] + core, half, grad_query)
            if pending is not None and pending[1] < 3:
                pass_keys(*pending)
            pending = (half, i)
            if pending == (1, 2):
                finish_values()
    total[0] = jnp.transpose(grad_query).astype(BF16)

    for j in range(4):
        start_back(0, j)
    for half in range(2):
        low = half * half_rows
        high = low + half_rows
        summed = pass_keys(half, 3)
        for i in range(3):
            arrived(half_of(in_k, i, half), mk_recv.at[half, i])
            summed += in_k[i, low:high].astype(F32)
        total[1, low:high] = summed.astype(BF16)
        for j in range(2 * half, 2 * half + 2):
            start_back(1, j)

    start_windows(1, 0, 1)

    def put_raw_grad(which, i, upstream_grad):
        unit, inv = unit_rows(raw[1 - which, :, i * HS : (i + 1) * HS])
        dall[which, :, i * HS : (i + 1) * HS] = unit_back(upstream_grad.astype(F32), unit, inv).astype(BF16)

    for i in range(HEADS):
        arrived(back.at[0, i], b_recv.at[0, i])
        put_raw_grad(0, i, back[0, i])
    grad_normed = lax.dot_general(dall[0], wq_ref[...], LAST_BOTH, preferred_element_type=F32)
    for i in range(HEADS):
        arrived(back.at[2, i], b_recv.at[2, i])
        dall[2, :, i * HS : (i + 1) * HS] = back[2, i]
    grad_normed += lax.dot_general(dall[2], wv_ref[...], LAST_BOTH, preferred_element_type=F32)
    for i in range(HEADS):
        arrived(back.at[1, i], b_recv.at[1, i])
        put_raw_grad(1, i, back[1, i])
    grad_normed += lax.dot_general(dall[1], wk_ref[...], LAST_BOTH, preferred_element_type=F32)
    gained = grad_normed * gain
    unit_feats = feats * inv_rms
    feature_grad = inv_rms * (gained - unit_feats * jnp.mean(unit_feats * gained, axis=1, keepdims=True))
    feature_grad = feature_grad.astype(BF16)
    fg_out[...] = feature_grad
    for i in range(2):
        for k in range(3):
            fgs[i, k] = feature_grad[:, i * HALF + k * 128 : i * HALF + (k + 1) * 128]

    def g_slot(k, xx, cc):
        return fgb.at[k, pl.ds(pl.multiple_of((2 * xx + cc) * TOK, TOK), TOK)]

    for k in range(3):
        for i, (where, cc, slot_at) in enumerate(
            (
                (right, core, core),
                (left, core, 2 + core),
                (right_twin, 1 - core, core),
                (left_twin, 1 - core, 2 + core),
                (twin, 1 - core, 6),
            )
        ):
            send(fgs.at[cc, k], g_slot(k, x, core), g_send.at[k, i], g_recv.at[k, slot_at], where)
        if k == 2:
            for i, (where, cc) in enumerate(((far, core), (far_twin, 1 - core))):
                send(fgs.at[cc, k], g_slot(k, x, core), g_send.at[k, 5 + i], g_recv.at[k, 4 + core], where)
        fgb[k, pl.ds(pl.multiple_of(me * TOK, TOK), TOK)] = fgs[core, k]
    windows_on(1, 0, 1)

    def gather_on(k):
        arrived(g_slot(k, xl, 0), g_recv.at[k, 0])
        send(g_slot(k, xl, 0), g_slot(k, xl, 0), g_send.at[k, 5], g_recv.at[k, 4], right)
        arrived(g_slot(k, xr, 1), g_recv.at[k, 3])
        send(g_slot(k, xr, 1), g_slot(k, xr, 1), g_send.at[k, 6], g_recv.at[k, 5], left)

    def sum_chunk(k):
        arrived(g_slot(k, xl, 1), g_recv.at[k, 1])
        arrived(g_slot(k, xr, 0), g_recv.at[k, 2])
        arrived(g_slot(k, x, 1 - core), g_recv.at[k, 6])
        arrived(g_slot(k, xo, 0), g_recv.at[k, 4])
        arrived(g_slot(k, xo, 1), g_recv.at[k, 5])
        terms = jnp.dot(wbuf[...].reshape(3 * QUARTER, 8 * TOK), fgb[k], preferred_element_type=F32) * (1.0 / (2 * NZ))
        for b in range(NY):
            taps = [terms[i * QUARTER + b * SPAN : i * QUARTER + (b + 1) * SPAN] for i in range(3)]
            rows = jnp.concatenate(taps + [jnp.zeros((PAD - 3 * SPAN, 128), F32)], axis=0).astype(BF16)
            for i, (by_z, at_tile) in enumerate(TILES[k]):
                tile = rows[16 * i : 16 * (i + 1)]
                if by_z:
                    tiles_z[at_tile, b] = tile
                else:
                    tiles_y[b, at_tile] = tile
        of_y = [at_tile for by_z, at_tile in TILES[k] if not by_z]
        some = pl.ds(of_y[0], len(of_y))
        for i in range(1, NY):
            to_y = lax.rem(y + i, NY)
            send(tiles_y.at[to_y, some], yb1.at[y, some], t_send.at[k, i], t_recv.at[k, y], on_y[i - 1])
        yb1[y, some] = tiles_y[y, some]
        for by_z, at_tile in TILES[k]:
            if by_z:

                @pl.when(z != at_tile)
                def _():
                    to_owner(at_tile).start()

                @pl.when(z == at_tile)
                def _():
                    zb1[z] = tiles_z[at_tile]

    def to_owner(at_tile):
        return copy(tiles_z.at[at_tile], zb1.at[z], tz_send.at[at_tile], tz_recv.at[z], (seq, 2 * at_tile + core))

    def added(ref):
        out = ref[0].astype(F32)
        for i in range(1, 8):
            out += ref[i].astype(F32)
        return out

    @pl.when(z == NZ - 1)
    def _():
        zb1[...] = jnp.zeros_like(zb1)

    gather_on(0)
    gather_on(1)
    got_windows(0, 1, 2)
    got_windows(1, 0, 1)
    sum_chunk(0)
    arrived(g_slot(2, xl, 0), g_recv.at[2, 0])
    arrived(g_slot(2, xr, 1), g_recv.at[2, 3])
    sum_chunk(1)
    sum_chunk(2)
    for i in range(1, NY):
        from_y = lax.rem(y + i, NY)
        for k in range(3):
            of_y = [at_tile for by_z, at_tile in TILES[k] if not by_z]
            arrived(yb1.at[from_y, pl.ds(of_y[0], len(of_y))], t_recv.at[k, from_y])
    s1[...] = added(yb1).astype(BF16)
    for i in range(1, 8):
        to_z = lax.rem(z + i, NZ)
        send(s1.at[to_z], zb2.at[z], u_send.at[0, i], u_recv.at[0, z], on_z[i - 1])

    @pl.when(z < NZ - 1)
    def _():
        for i in range(1, 8):
            from_z = lax.rem(z + i, NZ)
            arrived(zb1.at[from_z], tz_recv.at[from_z])

    s2[...] = added(zb1).astype(BF16)
    for i in range(1, 8):
        to_y = lax.rem(y + i, NY)
        send(s2.at[to_y], yb2.at[y], u_send.at[1, i], u_recv.at[1, y], on_y[i - 1])
    zb2[z] = s1[z]
    yb2[y] = s2[y]
    for i in range(1, 8):
        from_z = lax.rem(z + i, NZ)
        arrived(zb2.at[from_z], u_recv.at[0, from_z])
    fin[z, 0] = added(zb2).astype(BF16)
    for i in range(1, 8):
        from_y = lax.rem(y + i, NY)
        arrived(yb2.at[from_y], u_recv.at[1, from_y])
    fin[z, 1] = added(yb2).astype(BF16)
    for i in range(1, 8):
        send(fin.at[z], fin.at[z], f_send.at[i], f_recv.at[z], on_z[i - 1])
    for i in range(1, 8):
        from_z = lax.rem(z + i, NZ)
        arrived(fin.at[from_z], f_recv.at[from_z])
    send(fin, fin_sib, c_sem.at[0], c_sem.at[1], twin)
    arrived(fin_sib, c_sem.at[1])
    for half in range(2):
        mine = jnp.where(core == half, fin[...].astype(F32), fin_sib[...].astype(F32))
        wide = []
        for i in range(PAD // 16):
            row = [TILES[k][i] for k in range(3)]
            wide.append(jnp.concatenate([mine[at_tile, int(by_z)] for by_z, at_tile in row], axis=1))
        wide = jnp.concatenate(wide, axis=0)
        for k in range(3):
            cg_out[k, :, half * HALF : (half + 1) * HALF] = wide[k * SPAN : (k + 1) * SPAN]

    for one in sends:
        one.wait_send()
    for at_tile in range(NZ - 1):

        @pl.when(z != at_tile)
        def _():
            to_owner(at_tile).wait_send()


def publish(fg_in, cg_in, fg_out, cg_out):
    fg_out[0] = fg_in[...]
    cg_out[...] = cg_in[...]


def on_device(input_rows, features, norm_gain, w_query, w_key, w_value, temper, head_grads):
    vmem, hbm = pl.BlockSpec(memory_space=pltpu.VMEM), pl.BlockSpec(memory_space=pl.ANY)
    dma = pltpu.SemaphoreType.DMA

    def scratch(*shape, dtype=BF16):
        return pltpu.VMEM(shape, dtype)

    fg, cg = pl.pallas_call(
        kernel,
        out_shape=(
            jax.ShapeDtypeStruct((TOK, CH), BF16),
            jax.ShapeDtypeStruct((3, SPAN, CH), F32),
        ),
        in_specs=[hbm] * 8,
        out_specs=(vmem, vmem),
        scratch_shapes=[
            scratch(2 * TOK, CH),
            scratch(TOK, CH),
            scratch(CH, dtype=F32),
            scratch(CH, HEADS * HS),
            scratch(CH, HEADS * HS),
            scratch(CH, HEADS * HS),
            pltpu.SMEM((HEADS,), F32),
            scratch(TOK, HEADS * HS),
            scratch(16, CH),
            scratch(4, HEADS, TOK, HS),
            scratch(8, QROWS, HS),
            scratch(8, QROWS, HS),
            scratch(2, QROWS, HS),
            scratch(2, TOK, HEADS * HS, dtype=F32),
            scratch(NX, 3, QUARTER, TOK),
            scratch(3, QUARTER, 8 * TOK),
            scratch(8, QROWS, QROWS, dtype=F32),
            scratch(8, QROWS, QROWS, dtype=F32),
            scratch(8, QROWS, HS),
            scratch(8, QROWS, HS),
            scratch(NX, QROWS, HS),
            scratch(NX, QROWS, HS),
            scratch(3, QROWS, HS),
            scratch(3, QROWS, HS),
            scratch(3, QROWS, HS),
            scratch(3, QROWS, HS),
            scratch(3, QROWS, HS),
            scratch(3, HEADS, TOK, HS),
            scratch(3, TOK, HEADS * HS),
            scratch(2, 3, TOK, 128),
            scratch(3, 8 * TOK, 128),
            scratch(NY, 8, 16, 128),
            scratch(NZ, NY, 16, 128),
            scratch(NY, 8, 16, 128),
            scratch(NZ, 8, 16, 128),
            scratch(8, 16, 128),
            scratch(8, 16, 128),
            scratch(NZ, 16, 128),
            scratch(NY, 16, 128),
            scratch(NZ, 2, 16, 128),
            scratch(NZ, 2, 16, 128),
            dma((2,)),
            dma((4, 4)), dma((4, 4)),
            dma((2, 19)), dma((2, 19)),
            dma((2, 7)), dma((2, 7)),
            dma((4,)), dma((4,)),
            dma((2, 4)), dma((2, 4)),
            dma((3,)), dma((3,)),
            dma((2, 3)), dma((2, 3)),
            dma((3, 4)), dma((3, 4)),
            dma((3, 7)), dma((3, 7)),
            dma((3, 8)), dma((3, 8)),
            dma((8,)), dma((8,)),
            dma((2, 8)), dma((2, 8)),
            dma((8,)), dma((8,)),
            dma((2,)),
            dma((8,)),
        ],
        compiler_params=pltpu.CompilerParams(
            collective_id=0, has_side_effects=True, vmem_limit_bytes=56 * 1024 * 1024
        ),
    )(
        input_rows[0], features[0], norm_gain, w_query, w_key, w_value, temper, head_grads[0],
    )
    return pl.pallas_call(
        publish,
        out_shape=(
            jax.ShapeDtypeStruct((1, TOK, CH), BF16),
            jax.ShapeDtypeStruct((3, SPAN, CH), F32),
        ),
        in_specs=[vmem, vmem],
        out_specs=(vmem, vmem),
    )(fg, cg)


def solution(mesh):
    return jax.shard_map(
        on_device,
        mesh=mesh,
        in_specs=(
            P("dp", "seq", None),
            P("dp", "seq", None),
            P(),
            P(),
            P(),
            P(),
            P(),
            P("dp", "seq", None),
        ),
        out_specs=(P("dp", "seq", None), P(None, "seq", None)),
        check_vma=False,
    )
```

```python
import math

import jax
import jax.numpy as jnp
from jax import lax
from jax.experimental import pallas as pl
from jax.experimental.pallas import tpu as pltpu
from jax.sharding import PartitionSpec as P

EPSILON = 1e-06
LAST_BOTH = (((1,), (1,)), ((), ()))
FIRST_BOTH = (((0,), (0,)), ((), ()))
MESH = pl.DeviceIdType.MESH
BF16, F32 = jnp.bfloat16, jnp.float32

NX, NY, NZ = 4, 8, 8
TOK, CH, HEADS, HS = 128, 768, 4, 128
QROWS = 512
SPAN = CH // (NX * NY)
HALF = CH // 2
QUARTER = CH // NX
TILES = (
    ((False, 0), (False, 1), (False, 2), (True, 3)),
    ((False, 3), (False, 4), (True, 0), (True, 2), (True, 5)),
    ((False, 5), (False, 6), (True, 1), (True, 4), (True, 6)),
)
N_TILES = 7


def unit_rows(raw):
    inv = lax.rsqrt(jnp.mean(raw * raw, axis=-1, keepdims=True) + EPSILON)
    return raw * inv, inv


def unit_back(upstream, unit, inv):
    return inv * (upstream - unit * jnp.mean(unit * upstream, axis=-1, keepdims=True))


def kernel(
    rows_hbm, feat_hbm, gain_hbm, wq_hbm, wk_hbm, wv_hbm, temper_hbm, hg_hbm,
    fg_out, own_out, twin_out,
    rows_ref, feat_ref, gain_ref, wq_ref, wk_ref, wv_ref, temper_ref, hg_ref, prev, outgoing, keys, vals, qg, raw, wt, wbuf, e_buf, gp_buf, dv, dk, sib_v, sib_k, st_v, st_k, in_v, in_k,
    total, back, dall, fgs, fgb, tiles_y, tiles_z, yb1, zb1, s1, s2, zb2, yb2, fin, fin_sib,
    prev_sem, a_send, a_recv, k_send, k_recv, w_send, w_recv, sv_send, sv_recv, sk_send, sk_recv,
    mv_send, mv_recv, mk_send, mk_recv, b_send, b_recv, g_send, g_recv, t_send, t_recv, tz_send, tz_recv, u_send, u_recv, f_send, f_recv, c_sem, in_sem,
):
    seq, dp = lax.axis_index("seq"), lax.axis_index("dp")
    x, y = lax.div(seq, NY), lax.rem(seq, NY)
    z, core = lax.div(dp, 2), lax.rem(dp, 2)
    n_seq = NX * NY
    xr, xl, xo = lax.rem(x + 1, NX), lax.rem(x + NX - 1, NX), lax.rem(x + 2, NX)
    sib = dp + 1 - 2 * core
    part_y, head = lax.rem(y, 2), lax.div(y, 2)
    me = 2 * x + core

    def at(xx, yy):
        return xx * NY + yy

    def copy(src, dst, send, recv, where):
        return pltpu.make_async_remote_copy(
            src_ref=src, dst_ref=dst, send_sem=send, recv_sem=recv, device_id=where, device_id_type=MESH
        )

    sends = []

    def send(src, dst, send_sem, recv_sem, where):
        one = copy(src, dst, send_sem, recv_sem, where)
        one.start()
        sends.append(one)
        return one

    def arrived(dst, recv):
        copy(dst, dst, recv, recv, (seq, sib)).wait_recv()

    def rows_of(ref, start, size):
        return ref.at[pl.ds(pl.multiple_of(start, 16), size)]

    servers = [(at(x, 2 * i + core), 2 * z + 1 - lax.rem(y, 2)) for i in range(HEADS)]
    owners = [(at(x, 2 * j + 1 - core), 2 * z + part_y) for j in range(4)]
    ring_next, ring_prev = (lax.rem(seq + 1, n_seq), dp), (lax.rem(seq + n_seq - 1, n_seq), dp)
    right, left, twin, far = (at(xr, y), dp), (at(xl, y), dp), (seq, sib), (at(xo, y), dp)
    right_twin, left_twin, far_twin = (at(xr, y), sib), (at(xl, y), sib), (at(xo, y), sib)
    on_y = [(at(x, lax.rem(y + i, NY)), dp) for i in range(1, NY)]
    on_z = [(seq, lax.rem(dp + 2 * i, 2 * NZ)) for i in range(1, NZ)]

    barrier = pltpu.get_barrier_semaphore()
    partners = servers + owners + [ring_next, ring_prev, right, left, twin, far, right_twin, left_twin, far_twin] + on_y + on_z
    for where in partners:
        pl.semaphore_signal(barrier, inc=1, device_id=where, device_id_type=MESH)

    staged = []
    for i, (src, dst) in enumerate(
        (
            (feat_hbm, feat_ref), (gain_hbm, gain_ref), (wk_hbm, wk_ref), (temper_hbm, temper_ref),
            (wv_hbm, wv_ref), (hg_hbm, hg_ref), (rows_hbm, rows_ref), (wq_hbm, wq_ref),
        )
    ):
        staged.append(pltpu.make_async_copy(src, dst, in_sem.at[i]))
        staged[i].start()

    for one in staged[:4]:
        one.wait()
    feats = feat_ref[...].astype(F32)
    inv_rms = lax.rsqrt(jnp.mean(feats * feats, axis=1, keepdims=True) + EPSILON)
    gain = gain_ref[...].reshape(1, CH)
    normed = (feats * inv_rms * gain).astype(BF16)
    slot = lax.div(y, 2)
    their_me = 2 * x + 1 - lax.rem(y, 2)

    def start_heads(kind, to):
        started = []
        for i in range(HEADS):
            started.append(copy(outgoing.at[kind, i], to, a_send.at[kind, i], a_recv.at[kind, slot], servers[i]))
            started[i].start()
        return started

    def wait_heads(started):
        for one in started:
            one.wait_send()

    def project(which, w_ref):
        raw[which] = jnp.dot(normed, w_ref[...], preferred_element_type=F32)
        for i in range(HEADS):
            outgoing[which, i] = unit_rows(raw[which, :, i * HS : (i + 1) * HS])[0].astype(BF16)

    project(0, wk_ref)
    pl.semaphore_wait(barrier, len(partners))
    slot_rows = pl.ds(pl.multiple_of(slot * TOK, TOK), TOK)
    sent = start_heads(0, keys.at[their_me, slot_rows])
    staged[6].wait()
    send(rows_ref.at[pl.ds(2 * TOK - 16, 16)], prev, prev_sem.at[0], prev_sem.at[1], ring_next)
    staged[4].wait()
    staged[5].wait()
    values = jnp.dot(normed, wv_ref[...], preferred_element_type=F32).astype(BF16)
    for i in range(HEADS):
        outgoing[2, i] = values[:, i * HS : (i + 1) * HS]
        outgoing[3, i] = hg_ref[:, i * HS : (i + 1) * HS]

    def chosen(rows, columns, first_tap):
        row = lax.broadcasted_iota(jnp.int32, (rows, columns), 0)
        lane = lax.broadcasted_iota(jnp.int32, (rows, columns), 1)
        return (row == 2 * lax.rem(lane, TOK) + lax.div(lane, TOK) + first_tap - 1).astype(F32).astype(BF16)

    def w_slot(first_tap, taps, xx, cc):
        return wbuf.at[pl.ds(first_tap, taps), :, pl.ds(pl.multiple_of((2 * xx + cc) * TOK, TOK), TOK)]

    def put_windows(tap, windows):
        for i in range(NX):
            wt[i, tap] = windows[i * QUARTER : (i + 1) * QUARTER].astype(BF16)
        wbuf[tap, :, pl.ds(pl.multiple_of(me * TOK, TOK), TOK)] = wt[x, tap]

    def start_windows(group, first_tap, taps):
        some = pl.ds(first_tap, taps)
        for i, (to_x, where) in enumerate(((xl, left), (xr, right), (xo, far), (x, twin))):
            src = wt.at[to_x, some]
            send(src, w_slot(first_tap, taps, x, core), w_send.at[group, i], w_recv.at[group, i], where)

    def windows_on(group, first_tap, taps):
        for i, from_x in enumerate((xr, xl, xo)):
            piece = w_slot(first_tap, taps, from_x, core)
            arrived(piece, w_recv.at[group, i])
            send(piece, piece, w_send.at[group, 4 + i], w_recv.at[group, 4 + i], twin)

    def got_windows(group, first_tap, taps):
        for i, from_x in enumerate((x, xr, xl, xo)):
            arrived(w_slot(first_tap, taps, from_x, 1 - core), w_recv.at[group, 3 + i])

    windows = lax.dot_general(rows_ref[...], chosen(2 * TOK, 2 * TOK, 1), FIRST_BOTH, preferred_element_type=F32)
    put_windows(1, windows[:, 0:TOK])
    put_windows(2, windows[:, TOK:])
    start_windows(0, 1, 2)
    wait_heads(sent)
    sends += start_heads(2, vals.at[their_me, slot_rows])
    staged[7].wait()
    project(1, wq_ref)
    arrived(prev, prev_sem.at[1])
    row = lax.broadcasted_iota(jnp.int32, (16, TOK), 0)
    lane = lax.broadcasted_iota(jnp.int32, (16, TOK), 1)
    first = ((row == 15) & (lane == 0) & (seq > 0)).astype(F32).astype(BF16)
    windows = lax.dot_general(rows_ref[...], chosen(2 * TOK, TOK, 0), FIRST_BOTH, preferred_element_type=F32)
    put_windows(0, windows + lax.dot_general(prev[...], first, FIRST_BOTH, preferred_element_type=F32))

    def chunk(ref, block, i):
        j = lax.rem(slot + (0, 1, 3, 2)[i], 4)
        return ref.at[block, pl.ds(pl.multiple_of(j * TOK, TOK), TOK)], j

    from_left, from_right, from_far = 2 * xl + core, 2 * xr + core, 2 * xo + core
    twin_me, twin_left, twin_right, twin_far = me + 1 - 2 * core, 2 * xl + 1 - core, 2 * xr + 1 - core, 2 * xo + 1 - core
    both = (keys, vals)

    def ring_own(t, i):
        mine, j = chunk(both[t], me, i)
        arrived(mine, a_recv.at[2 * t, j])
        for k, where in enumerate((right, left, twin)):
            send(mine, mine, k_send.at[t, 3 * i + k], k_recv.at[t, (0, 4, 12)[k] + i], where)

    def ring_on(t):
        for i, block, first_slot, onward in (
            (0, from_left, 0, right), (1, from_left, 0, right), (0, from_right, 4, None), (1, from_right, 4, None),
            (2, from_right, 4, left), (3, from_right, 4, left), (2, from_left, 0, None), (3, from_left, 0, None),
        ):
            piece, _ = chunk(both[t], block, i)
            arrived(piece, k_recv.at[t, first_slot + i])
            if onward is not None:
                send(piece, piece, k_send.at[t, 12 + i], k_recv.at[t, 8 + i], onward)
        for k, block in enumerate((from_left, from_right)):
            send(both[t].at[block], both[t].at[block], k_send.at[t, 16 + k], k_recv.at[t, 16 + k], twin)

    def ring_far(t):
        for i in range(4):
            arrived(chunk(both[t], from_far, i)[0], k_recv.at[t, 8 + i])
        send(both[t].at[from_far], both[t].at[from_far], k_send.at[t, 18], k_recv.at[t, 18], twin)

    def got_twin(t):
        for i in range(4):
            arrived(chunk(both[t], twin_me, i)[0], k_recv.at[t, 12 + i])

    def got_from_twin(t, k):
        arrived(both[t].at[(twin_left, twin_right, twin_far)[k]], k_recv.at[t, 16 + k])

    ring_own(0, 0)
    ring_own(0, 1)
    sends += start_heads(1, qg.at[0, slot_rows])
    ring_own(0, 2)
    ring_own(0, 3)
    sends += start_heads(3, qg.at[1, slot_rows])
    ring_own(1, 0)
    ring_own(1, 1)
    ring_own(1, 2)
    ring_own(1, 3)
    ring_on(0)

    for j in range(4):
        arrived(qg.at[0, pl.ds(j * TOK, TOK)], a_recv.at[1, j])
    factor = temper_ref[head] * (1.0 / math.sqrt(HS))

    def score_pass(block, exp_sum):
        scores = lax.dot_general(keys[block], qg[0], LAST_BOTH, preferred_element_type=F32)
        expo = jnp.exp2(scores * (factor * math.log2(math.e)))
        e_buf[block] = expo
        return exp_sum + jnp.sum(expo, axis=0, keepdims=True)

    def prob_grad(block, dot_sum):
        grad_prob = lax.dot_general(vals[block], qg[1], LAST_BOTH, preferred_element_type=F32)
        gp_buf[block] = grad_prob
        return dot_sum + jnp.sum(e_buf[block] * grad_prob, axis=0, keepdims=True)

    exp_sum = score_pass(me, jnp.zeros((1, QROWS), F32))
    got_twin(0)
    exp_sum = score_pass(twin_me, exp_sum)
    ring_on(1)
    exp_sum = score_pass(from_left, exp_sum)
    exp_sum = score_pass(from_right, exp_sum)
    ring_far(0)
    got_from_twin(0, 0)
    exp_sum = score_pass(twin_left, exp_sum)
    got_from_twin(0, 1)
    exp_sum = score_pass(twin_right, exp_sum)
    exp_sum = score_pass(from_far, exp_sum)
    for j in range(4):
        arrived(qg.at[1, pl.ds(j * TOK, TOK)], a_recv.at[3, j])
    dot_sum = prob_grad(me, jnp.zeros((1, QROWS), F32))
    got_twin(1)
    dot_sum = prob_grad(twin_me, dot_sum)
    got_from_twin(0, 2)
    exp_sum = score_pass(twin_far, exp_sum)
    inv_sum = 1.0 / exp_sum

    order = (xo, xr, xl, x)
    to = (far, right, left)

    def value_grad(block):
        prob = (e_buf[block] * inv_sum).astype(BF16)
        dv[block] = jnp.dot(prob, qg[1], preferred_element_type=F32).astype(BF16)

    def pass_values(i):
        arrived(sib_v.at[i], sv_recv.at[i])
        st_v[i] = (dv[2 * order[i] + core].astype(F32) + sib_v[i].astype(F32)).astype(BF16)
        send(st_v.at[i], in_v.at[i], mv_send.at[i], mv_recv.at[i], to[i])

    for i in range(NX):
        block = 2 * order[i] + 1 - core
        value_grad(block)
        send(dv.at[block], sib_v.at[i], sv_send.at[i], sv_recv.at[i], twin)
        value_grad(2 * order[i] + core)
        if i > 1:
            pass_values(i - 2)
    dot_sum = prob_grad(from_left, dot_sum)
    pass_values(2)
    dot_sum = prob_grad(from_right, dot_sum)
    ring_far(1)
    for k, other in enumerate((twin_left, twin_right)):
        got_from_twin(1, k)
        dot_sum = prob_grad(other, dot_sum)
    dot_sum = prob_grad(from_far, dot_sum)
    got_from_twin(1, 2)
    dot_sum = prob_grad(twin_far, dot_sum)
    windows_on(0, 1, 2)

    grad_dot = dot_sum * inv_sum
    inv_factor = inv_sum * factor
    half_rows = QROWS // 2

    def key_grad(block, half, grad_query):
        low = half * half_rows
        high = low + half_rows
        grad_score = (e_buf[block, low:high] * inv_factor * (gp_buf[block, low:high] - grad_dot)).astype(BF16)
        dk[block, low:high] = jnp.dot(grad_score, qg[0], preferred_element_type=F32).astype(BF16)
        keys_t = jnp.transpose(keys[block, low:high])
        return grad_query + jnp.dot(keys_t, grad_score, preferred_element_type=F32)

    def half_of(ref, i, half):
        return ref.at[i, pl.ds(half * half_rows, half_rows)]

    def pass_keys(half, i):
        low = half * half_rows
        high = low + half_rows
        arrived(half_of(sib_k, i, half), sk_recv.at[half, i])
        summed = dk[2 * order[i] + core, low:high].astype(F32) + sib_k[i, low:high].astype(F32)
        if i < 3:
            st_k[i, low:high] = summed.astype(BF16)
            send(half_of(st_k, i, half), half_of(in_k, i, half), mk_send.at[half, i], mk_recv.at[half, i], to[i])
        return summed

    def start_back(kind, j):
        src = total.at[kind, pl.ds(j * TOK, TOK)]
        send(src, back.at[kind, head], b_send.at[kind, j], b_recv.at[kind, head], owners[j])

    def finish_values():
        arrived(sib_v.at[3], sv_recv.at[3])
        summed = dv[me].astype(F32) + sib_v[3].astype(F32)
        for i in range(3):
            arrived(in_v.at[i], mv_recv.at[i])
            summed += in_v[i].astype(F32)
        total[2] = summed.astype(BF16)
        for j in range(4):
            start_back(2, j)

    grad_query = jnp.zeros((HS, QROWS), F32)
    pending = []
    for half in range(2):
        for i in range(NX):
            block = 2 * order[i] + 1 - core
            grad_query = key_grad(block, half, grad_query)
            send(half_of(dk, block, half), half_of(sib_k, i, half), sk_send.at[half, i], sk_recv.at[half, i], twin)
            grad_query = key_grad(2 * order[i] + core, half, grad_query)
            if i < 3:
                pending.append((half, i))
            if len(pending) > 2:
                pass_keys(*pending.pop(0))
    for one in pending:
        pass_keys(*one)
    total[0] = jnp.transpose(grad_query).astype(BF16)

    for j in range(4):
        start_back(0, j)
    finish_values()
    for half in range(2):
        low = half * half_rows
        high = low + half_rows
        summed = pass_keys(half, 3)
        for i in range(3):
            arrived(half_of(in_k, i, half), mk_recv.at[half, i])
            summed += in_k[i, low:high].astype(F32)
        total[1, low:high] = summed.astype(BF16)
        for j in range(2 * half, 2 * half + 2):
            start_back(1, j)

    start_windows(1, 0, 1)

    def put_raw_grad(which, i, upstream_grad):
        unit, inv = unit_rows(raw[1 - which, :, i * HS : (i + 1) * HS])
        dall[which, :, i * HS : (i + 1) * HS] = unit_back(upstream_grad.astype(F32), unit, inv).astype(BF16)

    for i in range(HEADS):
        arrived(back.at[0, i], b_recv.at[0, i])
        put_raw_grad(0, i, back[0, i])
    grad_normed = lax.dot_general(dall[0], wq_ref[...], LAST_BOTH, preferred_element_type=F32)
    for i in range(HEADS):
        arrived(back.at[2, i], b_recv.at[2, i])
        dall[2, :, i * HS : (i + 1) * HS] = back[2, i]
    grad_normed += lax.dot_general(dall[2], wv_ref[...], LAST_BOTH, preferred_element_type=F32)
    for i in range(HEADS):
        arrived(back.at[1, i], b_recv.at[1, i])
        put_raw_grad(1, i, back[1, i])
    grad_normed += lax.dot_general(dall[1], wk_ref[...], LAST_BOTH, preferred_element_type=F32)
    gained = grad_normed * gain
    unit_feats = feats * inv_rms
    feature_grad = inv_rms * (gained - unit_feats * jnp.mean(unit_feats * gained, axis=1, keepdims=True))
    feature_grad = feature_grad.astype(BF16)
    fg_out[...] = feature_grad
    for i in range(2):
        for k in range(3):
            fgs[i, k] = feature_grad[:, i * HALF + k * 128 : i * HALF + (k + 1) * 128]

    def g_slot(k, xx, cc):
        return fgb.at[k, pl.ds(pl.multiple_of((2 * xx + cc) * TOK, TOK), TOK)]

    for k in range(3):
        for i, (where, cc, slot_at) in enumerate(
            (
                (right, core, core),
                (left, core, 2 + core),
                (right_twin, 1 - core, core),
                (left_twin, 1 - core, 2 + core),
                (twin, 1 - core, 6),
            )
        ):
            send(fgs.at[cc, k], g_slot(k, x, core), g_send.at[k, i], g_recv.at[k, slot_at], where)
        if k == 2:
            for i, (where, cc) in enumerate(((far, core), (far_twin, 1 - core))):
                send(fgs.at[cc, k], g_slot(k, x, core), g_send.at[k, 5 + i], g_recv.at[k, 4 + core], where)
        fgb[k, pl.ds(pl.multiple_of(me * TOK, TOK), TOK)] = fgs[core, k]
    windows_on(1, 0, 1)

    def gather_on(k):
        arrived(g_slot(k, xl, 0), g_recv.at[k, 0])
        send(g_slot(k, xl, 0), g_slot(k, xl, 0), g_send.at[k, 5], g_recv.at[k, 4], right)
        arrived(g_slot(k, xr, 1), g_recv.at[k, 3])
        send(g_slot(k, xr, 1), g_slot(k, xr, 1), g_send.at[k, 6], g_recv.at[k, 5], left)

    def sum_chunk(k, before):
        arrived(g_slot(k, xl, 1), g_recv.at[k, 1])
        arrived(g_slot(k, xr, 0), g_recv.at[k, 2])
        arrived(g_slot(k, x, 1 - core), g_recv.at[k, 6])
        arrived(g_slot(k, xo, 0), g_recv.at[k, 4])
        arrived(g_slot(k, xo, 1), g_recv.at[k, 5])
        terms = jnp.dot(wbuf[...].reshape(3 * QUARTER, 8 * TOK), fgb[k], preferred_element_type=F32) * (1.0 / (2 * NZ))
        after = []
        for b in range(NY):
            taps = [terms[i * QUARTER + b * SPAN : i * QUARTER + (b + 1) * SPAN] for i in range(3)]
            rows = jnp.concatenate(taps, axis=0)
            tiles = [rows[16 * i : 16 * (i + 1)] for i in range(4)]
            after.append(rows[64:72])
            if k == 1:
                tiles.append(jnp.concatenate([before[b], rows[64:72]], axis=0))
            elif k == 2:
                tiles.append(jnp.concatenate([rows[64:72], jnp.zeros((8, 128), F32)], axis=0))
            for tile, (by_z, at_tile) in zip(tiles, TILES[k]):
                if by_z:
                    tiles_z[at_tile, b] = tile.astype(BF16)
                else:
                    tiles_y[b, at_tile] = tile.astype(BF16)
        of_y = [at_tile for by_z, at_tile in TILES[k] if not by_z]
        some = pl.ds(of_y[0], len(of_y))
        for i in range(1, NY):
            to_y = lax.rem(y + i, NY)
            send(tiles_y.at[to_y, some], yb1.at[y, some], t_send.at[k, i], t_recv.at[k, y], on_y[i - 1])
        yb1[y, some] = tiles_y[y, some]
        for by_z, at_tile in TILES[k]:
            if by_z:

                @pl.when(z != at_tile)
                def _():
                    to_owner(at_tile).start()

                @pl.when(z == at_tile)
                def _():
                    zb1[z] = tiles_z[at_tile]

        return after

    def to_owner(at_tile):
        return copy(tiles_z.at[at_tile], zb1.at[z], tz_send.at[at_tile], tz_recv.at[z], (seq, 2 * at_tile + core))

    def added(ref):
        out = ref[0].astype(F32)
        for i in range(1, 8):
            out += ref[i].astype(F32)
        return out

    @pl.when(z == NZ - 1)
    def _():
        zb1[...] = jnp.zeros_like(zb1)

    gather_on(0)
    gather_on(1)
    got_windows(0, 1, 2)
    got_windows(1, 0, 1)
    halves = sum_chunk(0, None)
    arrived(g_slot(2, xl, 0), g_recv.at[2, 0])
    arrived(g_slot(2, xr, 1), g_recv.at[2, 3])
    sum_chunk(1, halves)
    sum_chunk(2, None)
    for i in range(1, NY):
        from_y = lax.rem(y + i, NY)
        for k in range(3):
            of_y = [at_tile for by_z, at_tile in TILES[k] if not by_z]
            arrived(yb1.at[from_y, pl.ds(of_y[0], len(of_y))], t_recv.at[k, from_y])
    s1[0:N_TILES] = added(yb1).astype(BF16)
    s1[N_TILES] = jnp.zeros((16, 128), BF16)
    for i in range(1, 8):
        to_z = lax.rem(z + i, NZ)
        send(s1.at[to_z], zb2.at[z], u_send.at[0, i], u_recv.at[0, z], on_z[i - 1])

    @pl.when(z < NZ - 1)
    def _():
        for i in range(1, 8):
            from_z = lax.rem(z + i, NZ)
            arrived(zb1.at[from_z], tz_recv.at[from_z])

    s2[...] = added(zb1).astype(BF16)
    for i in range(1, 8):
        to_y = lax.rem(y + i, NY)
        send(s2.at[to_y], yb2.at[y], u_send.at[1, i], u_recv.at[1, y], on_y[i - 1])
    zb2[z] = s1[z]
    yb2[y] = s2[y]
    for i in range(1, 8):
        from_z = lax.rem(z + i, NZ)
        arrived(zb2.at[from_z], u_recv.at[0, from_z])
    fin[z, 0] = added(zb2).astype(BF16)
    for i in range(1, 8):
        from_y = lax.rem(y + i, NY)
        arrived(yb2.at[from_y], u_recv.at[1, from_y])
    fin[z, 1] = added(yb2).astype(BF16)
    for i in range(1, 8):
        send(fin.at[z], fin.at[z], f_send.at[i], f_recv.at[z], on_z[i - 1])
    for i in range(1, 8):
        from_z = lax.rem(z + i, NZ)
        arrived(fin.at[from_z], f_recv.at[from_z])
    send(fin, fin_sib, c_sem.at[0], c_sem.at[1], twin)
    arrived(fin_sib, c_sem.at[1])
    own_out[...] = fin[...]
    twin_out[...] = fin_sib[...]

    for one in sends:
        one.wait_send()
    for at_tile in range(NZ - 1):

        @pl.when(z != at_tile)
        def _():
            to_owner(at_tile).wait_send()


def publish(fg_in, own, twin, fg_out, cg_out):
    fg_out[0] = fg_in[...]
    core = lax.rem(lax.axis_index("dp"), 2)
    for half in range(2):
        mine = jnp.where(core == half, own[...].astype(F32), twin[...].astype(F32))
        tiles = [[mine[at_tile, int(by_z)] for by_z, at_tile in row] for row in TILES]
        last = (tiles[1][4][0:8], tiles[1][4][8:16], tiles[2][4][0:8])
        wide = [jnp.concatenate([tiles[k][i] for k in range(3)], axis=1) for i in range(4)]
        wide = jnp.concatenate(wide + [jnp.concatenate(last, axis=1)], axis=0)
        for k in range(3):
            cg_out[k, :, half * HALF : (half + 1) * HALF] = wide[k * SPAN : (k + 1) * SPAN]


def on_device(input_rows, features, norm_gain, w_query, w_key, w_value, temper, head_grads):
    vmem, hbm = pl.BlockSpec(memory_space=pltpu.VMEM), pl.BlockSpec(memory_space=pl.ANY)
    dma = pltpu.SemaphoreType.DMA

    def scratch(*shape, dtype=BF16):
        return pltpu.VMEM(shape, dtype)

    results = pl.pallas_call(
        kernel,
        out_shape=(
            jax.ShapeDtypeStruct((TOK, CH), BF16),
            jax.ShapeDtypeStruct((NZ, 2, 16, 128), BF16),
            jax.ShapeDtypeStruct((NZ, 2, 16, 128), BF16),
        ),
        in_specs=[hbm] * 8,
        out_specs=(vmem, vmem, vmem),
        scratch_shapes=[
            scratch(2 * TOK, CH),
            scratch(TOK, CH),
            scratch(CH, dtype=F32),
            scratch(CH, HEADS * HS),
            scratch(CH, HEADS * HS),
            scratch(CH, HEADS * HS),
            pltpu.SMEM((HEADS,), F32),
            scratch(TOK, HEADS * HS),
            scratch(16, CH),
            scratch(4, HEADS, TOK, HS),
            scratch(8, QROWS, HS),
            scratch(8, QROWS, HS),
            scratch(2, QROWS, HS),
            scratch(2, TOK, HEADS * HS, dtype=F32),
            scratch(NX, 3, QUARTER, TOK),
            scratch(3, QUARTER, 8 * TOK),
            scratch(8, QROWS, QROWS, dtype=F32),
            scratch(8, QROWS, QROWS, dtype=F32),
            scratch(8, QROWS, HS),
            scratch(8, QROWS, HS),
            scratch(NX, QROWS, HS),
            scratch(NX, QROWS, HS),
            scratch(3, QROWS, HS),
            scratch(3, QROWS, HS),
            scratch(3, QROWS, HS),
            scratch(3, QROWS, HS),
            scratch(3, QROWS, HS),
            scratch(3, HEADS, TOK, HS),
            scratch(3, TOK, HEADS * HS),
            scratch(2, 3, TOK, 128),
            scratch(3, 8 * TOK, 128),
            scratch(NY, N_TILES, 16, 128),
            scratch(N_TILES, NY, 16, 128),
            scratch(NY, N_TILES, 16, 128),
            scratch(NZ, 8, 16, 128),
            scratch(8, 16, 128),
            scratch(8, 16, 128),
            scratch(NZ, 16, 128),
            scratch(NY, 16, 128),
            scratch(NZ, 2, 16, 128),
            scratch(NZ, 2, 16, 128),
            dma((2,)),
            dma((4, 4)), dma((4, 4)),
            dma((2, 19)), dma((2, 19)),
            dma((2, 7)), dma((2, 7)),
            dma((4,)), dma((4,)),
            dma((2, 4)), dma((2, 4)),
            dma((3,)), dma((3,)),
            dma((2, 3)), dma((2, 3)),
            dma((3, 4)), dma((3, 4)),
            dma((3, 7)), dma((3, 7)),
            dma((3, 8)), dma((3, 8)),
            dma((8,)), dma((8,)),
            dma((2, 8)), dma((2, 8)),
            dma((8,)), dma((8,)),
            dma((2,)),
            dma((8,)),
        ],
        compiler_params=pltpu.CompilerParams(
            collective_id=0, has_side_effects=True, vmem_limit_bytes=56 * 1024 * 1024
        ),
    )(
        input_rows[0], features[0], norm_gain, w_query, w_key, w_value, temper, head_grads[0],
    )
    return pl.pallas_call(
        publish,
        out_shape=(
            jax.ShapeDtypeStruct((1, TOK, CH), BF16),
            jax.ShapeDtypeStruct((3, SPAN, CH), F32),
        ),
        in_specs=[vmem, vmem, vmem],
        out_specs=(vmem, vmem),
    )(*results)


def solution(mesh):
    return jax.shard_map(
        on_device,
        mesh=mesh,
        in_specs=(
            P("dp", "seq", None),
            P("dp", "seq", None),
            P(),
            P(),
            P(),
            P(),
            P(),
            P("dp", "seq", None),
        ),
        out_specs=(P("dp", "seq", None), P(None, "seq", None)),
        check_vma=False,
    )
```
